32 devices in a mesh: strip: 8 (over y, x, core), branch: 4 (over z).
Axes of the slice: x: 2, y: 2, z: 4, core: 2. Of those that a mesh axis runs over, the one named last changes fastest.
Arguments:
- features: bfloat16 [64, 192, 512], P('strip'), may hold values from -6 to 6
- cotangent: bfloat16 [64, 192, 256], P('strip', None, 'branch'), may hold values from -6 to 6
- depth_weight: bfloat16 [4, 9, 512], P('branch'), may hold values from -2 to 2
- point_weight: bfloat16 [4, 512, 256], P('branch'), may hold values from -0.25 to 0.25
- joining_weight: bfloat16 [1024, 256], P('branch'), may hold values from -0.25 to 0.25
- branch_mask: int32 [4], replicated, may hold values from 0 to 1, as said below
Outputs:
- output: bfloat16 [64, 192, 256], P('strip', None, 'branch')
- joining_grad: float32 [1024, 256], P('branch')
- point_grad: float32 [4, 512, 256], P('branch')
- depth_grad: float32 [4, 9, 512], P('branch')
The draws below stay inside these ranges and needn't reach their ends.
Inputs may be any that keep to these rules, and one draw needn't show every extreme that they name: `branch_mask`: 1 marks an active branch; at least one branch is active and at least one is not.
All inputs are finite; a program needn't handle non-finite values.
Results may differ from the reference program's by a relative error of at most 0.014.
Values may be sent and summed in bfloat16 or wider, within the bound.
No kernel may reach another device: no remote copies, remote signals or barrier semaphores. Data moves between devices by JAX's collectives and lax.ppermute only.
A program may use at most 64 MiB of HBM per device.

```python
import math
import jax
import jax.numpy as jnp
from jax import lax

CIN = 512
CB = 256
DILATION_STEP = 6
WIDTH = 192
NB = 4
ROWS = 64


def draw_branch_mask(key, part):
    first_key, second_key = jax.random.split(jax.random.fold_in(key, 7))
    order = jax.random.permutation(first_key, NB)
    active_count = jax.random.randint(second_key, (), 1, NB)
    return (order < active_count).astype(jnp.int32)


def shard_levels(stream_key, extent, cuts, least, top_value):
    level, own = 1.0, jax.random.fold_in(stream_key, 6)
    for axis_at, blocks in cuts:
        draws = jnp.exp(jax.random.uniform(jax.random.fold_in(own, axis_at), (blocks,), jnp.float32, least / len(cuts), top_value / len(cuts)))
        level = level * jnp.repeat(draws, extent[axis_at] // blocks).reshape([-1 if axis == axis_at else 1 for axis in range(len(extent))])
    return level


def centred(key, extent, width, limit, pieces=(), kind=jnp.bfloat16):
    result = width * jax.random.normal(key, extent, jnp.float32)
    if pieces:
        result = result * shard_levels(key, extent, pieces, -0.22, 0.18)
    return jnp.clip(result, -limit, limit).astype(kind)


def setup_inputs(seed: int = 0) -> dict:
    key_list = jax.random.split(jax.random.key(seed), 7)
    return {
        "features": centred(key_list[0], (ROWS, WIDTH, CIN), 1.0, 6.0, ((0, 8),)),
        "cotangent": centred(key_list[1], (ROWS, WIDTH, CB), 1.0, 6.0, ((0, 8), (2, 4))),
        "depth_weight": centred(key_list[2], (NB, 9, CIN), 9 ** -0.5, 2.0, ((0, 4),)),
        "point_weight": centred(key_list[3], (NB, CIN, CB), CIN ** -0.5, 0.25, ((0, 4),)),
        "joining_weight": centred(key_list[4], (NB * CB, CB), (2 * CB) ** -0.5, 0.25, ((0, 4),)),
        "branch_mask": draw_branch_mask(jax.random.fold_in(key_list[6], 71), 0),
    }


tanh_coef = 0.7978845608
cubic_coef = 0.044715
slope_coef = 0.134145

def gelu_tanh(values):
    inner = jnp.tanh(tanh_coef * (values + cubic_coef * values * values * values))
    return 0.5 * values * (1.0 + inner)

def gelu_slope(values):
    inner = jnp.tanh(tanh_coef * (values + cubic_coef * values * values * values))
    return 0.5 * (1.0 + inner) + 0.5 * values * (1.0 - inner * inner) * tanh_coef * (1.0 + slope_coef * values * values)

def contract_rows(left, right):
    return lax.dot_general(left, right, (((0,), (0,)), ((), ())), preferred_element_type=jnp.float32)

def contract_cols(left, right):
    return lax.dot_general(left, right, (((1,), (1,)), ((), ())), preferred_element_type=jnp.float32)

def tap_piece(padded, dilation_rate, tap_index, row_count, col_count):
    row_start = tap_index // 3 * dilation_rate
    col_start = tap_index % 3 * dilation_rate
    return padded[row_start:row_start + row_count, col_start:col_start + col_count, :]

def branch_apply_forward(features, depth_row, point_row, mask_value, dilation_rate):
    row_count, col_count, chan_count = features.shape
    padded = jnp.pad(features, ((dilation_rate, dilation_rate), (dilation_rate, dilation_rate), (0, 0)))
    kernel = depth_row.astype(jnp.float32)
    summed = jnp.zeros(features.shape, jnp.float32)
    for tap_index in range(9):
        piece = tap_piece(padded, dilation_rate, tap_index, row_count, col_count)
        summed = summed + piece.astype(jnp.float32) * kernel[tap_index]
    dw_out = summed.astype(jnp.bfloat16).reshape(row_count * col_count, chan_count)
    pre_act = jnp.dot(dw_out, point_row, preferred_element_type=jnp.float32)
    branch_out = (gelu_tanh(pre_act) * mask_value).astype(jnp.bfloat16)
    return (padded, dw_out, pre_act, branch_out)

def reference(features, cotangent, depth_weight, point_weight, joining_weight, branch_mask):
    row_count, col_count, chan_count = features.shape
    pixel_count = row_count * col_count
    out_width = cotangent.shape[2]
    pixel_scale = 1.0 / math.sqrt(pixel_count)
    mask_values = branch_mask.astype(jnp.float32)
    joined_sum = jnp.zeros((pixel_count, out_width), jnp.float32)
    for branch_slot in range(NB):
        dilation_rate = (branch_slot + 1) * DILATION_STEP
        results = branch_apply_forward(features, depth_weight[branch_slot], point_weight[branch_slot], mask_values[branch_slot], dilation_rate)
        weight_rows = joining_weight[branch_slot * CB:(branch_slot + 1) * CB]
        joined_sum = joined_sum + jnp.dot(results[3], weight_rows, preferred_element_type=jnp.float32)
    output = gelu_tanh(joined_sum).astype(jnp.bfloat16).reshape(row_count, col_count, out_width)
    grad_joined = (cotangent.reshape(pixel_count, out_width).astype(jnp.float32) * gelu_slope(joined_sum)).astype(jnp.bfloat16)
    joining_parts = []
    point_parts = []
    depth_parts = []
    for branch_slot in range(NB):
        dilation_rate = (branch_slot + 1) * DILATION_STEP
        padded, dw_out, pre_act, branch_out = branch_apply_forward(features, depth_weight[branch_slot], point_weight[branch_slot], mask_values[branch_slot], dilation_rate)
        weight_rows = joining_weight[branch_slot * CB:(branch_slot + 1) * CB]
        joining_parts.append(contract_rows(branch_out, grad_joined) * pixel_scale)
        grad_branch = contract_cols(grad_joined, weight_rows) * mask_values[branch_slot]
        grad_pre = (grad_branch * gelu_slope(pre_act)).astype(jnp.bfloat16)
        point_parts.append(contract_rows(dw_out, grad_pre) * pixel_scale)
        depthwise_gradient = contract_cols(grad_pre, point_weight[branch_slot]).reshape(row_count, col_count, chan_count)
        tap_sums = []
        for tap_index in range(9):
            piece = tap_piece(padded, dilation_rate, tap_index, row_count, col_count)
            tap_sums.append(lax.optimization_barrier(jnp.sum(depthwise_gradient * piece.astype(jnp.float32), axis=(0, 1))) * pixel_scale)
        depth_parts.append(jnp.stack(tap_sums))
    return (output, jnp.concatenate(joining_parts, 0), jnp.stack(point_parts), jnp.stack(depth_parts))
```

```python
import functools
import math

import jax
import jax.numpy as jnp
from jax import lax
from jax.experimental import pallas as pl
from jax.experimental.pallas import tpu as pltpu
from jax.sharding import PartitionSpec as P

DILATION_STEP = 6
GROUP = 8
CHIPS = 4
SLOTS = 3

tanh_coef = 0.7978845608
cubic_coef = 0.044715
slope_coef = 0.134145

f32, bf16, i32 = jnp.float32, jnp.bfloat16, jnp.int32
VMEM = pl.BlockSpec(memory_space=pltpu.VMEM)
SMEM = pl.BlockSpec(memory_space=pltpu.SMEM)
ANY = pl.BlockSpec(memory_space=pl.ANY)


def gelu_both(values):
    square = values * values
    inner = jnp.tanh(tanh_coef * (values + cubic_coef * values * square))
    half = 0.5 * (1.0 + inner)
    slope = half + 0.5 * values * (1.0 - inner * inner) * tanh_coef * (1.0 + slope_coef * square)
    return values * half, slope


def dot(left, right, dims=((1,), (0,))):
    return lax.dot_general(left, right, (dims, ((), ())), preferred_element_type=f32)


def iota(shape, dim):
    return lax.broadcasted_iota(i32, shape, dim)


def one_hot(mask):
    return jnp.where(mask, 1.0, 0.0).astype(bf16)


class Plan:
    def __init__(self, row_count, col_count, chan_count, width, branches):
        self.rows, self.cols, self.chans, self.width, self.branches = row_count, col_count, chan_count, width, branches
        self.classes = DILATION_STEP
        self.run = col_count // DILATION_STEP
        self.work = col_count // (branches * CHIPS)
        self.taps_t = row_count // 2
        self.sub_rows = GROUP * self.taps_t
        self.pixels = self.sub_rows * self.work
        self.lanes = chan_count // 128
        self.window = max(self.segments(m)[5] for m in range(branches * CHIPS))
        self.piece = self.window * self.taps_t
        self.part = width // branches
        self.step_rows = DILATION_STEP // 2
        self.pad = -(-self.step_rows * branches // 16) * 16
        self.tall = self.pad + self.sub_rows + self.pad
        self.grad_rows = (width + chan_count) // GROUP
        self.join_rows = width // GROUP
        self.point_rows = chan_count // GROUP
        self.tile = 2 * self.work

    def segments(self, m):
        smaller, larger = (min, max) if isinstance(m, int) else (jnp.minimum, jnp.maximum)
        first = m * self.work
        klass = first // self.run
        start = first - klass * self.run
        length = smaller(self.work, self.run - start)
        low = larger(0, start - self.branches)
        size = smaller(self.run, start + length + self.branches) - low
        rest = self.work - length
        if isinstance(m, int):
            total = size + (min(self.run, rest + self.branches) if rest else 0)
        else:
            total = size + jnp.where(rest > 0, jnp.minimum(self.run, rest + self.branches), 0)
        return klass, start, length, low, size, total

    def column(self, m, w):
        klass, start, length, _, _, _ = self.segments(m)
        return jnp.where(w < length, self.classes * (start + w) + klass, self.classes * (w - length) + klass + 1)

    def window_column(self, m, j):
        klass, _, _, low, size, total = self.segments(m)
        inside = jnp.where(j < size, self.classes * (low + j) + klass, self.classes * (j - size) + klass + 1)
        return jnp.where(j < total, inside, -(1 << 20))

    def neighbour(self, segments, w, shift):
        _, start, length, low, size, _ = segments
        first = w < length
        place = jnp.where(first, start + w, w - length) + shift
        found = jnp.where(first, place - low, size + place)
        return jnp.where(jnp.logical_and(place >= 0, place < self.run), found, self.window)


def whereabouts():
    strip = lax.axis_index("strip") % GROUP
    return lax.axis_index("branch"), strip, strip // 2, strip % 2


def slots_of(mask_ref, branches):
    slots, count = [], 0
    for branch in range(branches):
        slots.append(jnp.minimum(count, SLOTS - 1) + 0 * mask_ref[branch])
        count = count + mask_ref[branch]
    return slots, count


def pick(values, index):
    result = values[0]
    for place in range(1, len(values)):
        result = jnp.where(index == place, values[place], result)
    return result


def spread_kernel(plan, features_ref, *out_refs):
    plane, _, chip, core = whereabouts()
    depth = plan.taps_t * plan.cols
    targets = []
    for hop in range(CHIPS):
        m = plane * CHIPS + (chip ^ hop)
        row = iota((plan.piece, 128), 0)
        column = plan.window_column(m, row // plan.taps_t)
        targets.append(column + (row % plan.taps_t) * plan.cols)
    target = jnp.concatenate(targets, 0)
    lane = iota(target.shape, 1)
    chosen = jnp.concatenate([one_hot(target == lane + 128 * k) for k in range(depth // 128)], 1)
    for flip in range(2):
        parity = core ^ flip
        rows = jnp.concatenate([features_ref[2 * t + parity] for t in range(plan.taps_t)], 0)
        found = dot(chosen, rows).astype(bf16)
        for hop in range(CHIPS):
            out_refs[2 * hop + flip][...] = found[hop * plan.piece:(hop + 1) * plan.piece]


def spread_features(plan, features):
    return pl.pallas_call(
        functools.partial(spread_kernel, plan),
        out_shape=[jax.ShapeDtypeStruct((plan.piece, plan.chans), bf16)] * GROUP,
        in_specs=[VMEM],
        out_specs=[VMEM] * GROUP,
        compiler_params=pltpu.CompilerParams(vmem_limit_bytes=40 << 20),
        name="spread_features",
    )(features)


def tile_columns(plan):
    blocks = []
    for chip in range(CHIPS):
        for plane in range(plan.branches):
            row = iota((plan.tile, 128), 0)
            column = plan.column(plane * CHIPS + chip, row // 2)
            blocks.append(column + (row % 2) * plan.cols)
    return jnp.concatenate(blocks, 0)


def tile_selector(plan):
    target = tile_columns(plan)
    lane = iota(target.shape, 1)
    return jnp.concatenate([one_hot(target == lane + 128 * k) for k in range(2 * plan.cols // 128)], 1)


def send_cotangent_kernel(plan, cotangent_ref, out_ref):
    chosen = tile_selector(plan)
    halves = []
    for parity in range(2):
        rows = []
        for low in range(2):
            pair = [cotangent_ref[2 * (2 * high + low) + parity].astype(f32) for high in range(2)]
            rows.append(jnp.concatenate(pair, 1))
        halves.append(jnp.concatenate(rows, 0))
    found = dot(chosen, jnp.concatenate(halves, 1).astype(bf16))
    for chip in range(CHIPS):
        for parity in range(2):
            for plane in range(plan.branches):
                at = (chip * plan.branches + plane) * plan.tile
                out_ref[(2 * chip + parity) * plan.branches + plane] = found[
                    at:at + plan.tile, parity * 128:(parity + 1) * 128
                ].astype(bf16)


def send_cotangent(plan, cotangent):
    return pl.pallas_call(
        functools.partial(send_cotangent_kernel, plan),
        out_shape=jax.ShapeDtypeStruct((GROUP * plan.branches, plan.tile, 128), bf16),
        in_specs=[VMEM],
        out_specs=VMEM,
        compiler_params=pltpu.CompilerParams(vmem_limit_bytes=40 << 20),
        name="send_cotangent",
    )(cotangent)


def place_output_kernel(plan, tiles_ref, out_ref):
    chosen = tile_selector(plan)
    halves = []
    for parity in range(2):
        blocks = []
        for chip in range(CHIPS):
            for plane in range(plan.branches):
                blocks.append(tiles_ref[(2 * chip + parity) * plan.branches + plane].astype(f32))
        halves.append(jnp.concatenate(blocks, 0))
    found = dot(chosen, jnp.concatenate(halves, 1).astype(bf16), ((0,), (0,))).astype(bf16)
    for parity in range(2):
        for high in range(2):
            for low in range(2):
                lane = parity * 128 + high * 64
                out_ref[2 * (2 * high + low) + parity] = found[low * plan.cols:(low + 1) * plan.cols, lane:lane + 64]


def place_output(plan, tiles):
    return pl.pallas_call(
        functools.partial(place_output_kernel, plan),
        out_shape=jax.ShapeDtypeStruct((plan.rows, plan.cols, plan.part), bf16),
        in_specs=[VMEM],
        out_specs=VMEM,
        compiler_params=pltpu.CompilerParams(vmem_limit_bytes=40 << 20),
        name="place_output",
    )(tiles)


def swap_halves(left, right):
    low = iota(left.shape, 1) < 64
    return (
        jnp.where(low, left, pltpu.roll(right, 64, 1)),
        jnp.where(low, pltpu.roll(left, 64, 1), right),
    )


def main_kernel(plan, scale, halo, mask_ref, cotangent_ref, *refs):
    count = GROUP + (2 if halo else 0)
    piece_refs, refs = refs[:GROUP], refs[count:] if not halo else refs[GROUP:]
    halo_refs, refs = (refs[:2], refs[2:]) if halo else ((), refs)
    branches, width, chans = plan.branches, plan.width, plan.chans
    depth_refs, refs = refs[:branches], refs[branches:]
    (point_ref, joining_ref), refs = refs[:2], refs[2:]
    mine_refs, refs = refs[:branches - 1], refs[branches - 1:]
    other_refs, refs = refs[:branches - 1], refs[branches - 1:]
    output_ref, keep_ref, send_ref = refs[:3]
    (pieces, halo_pieces, depth, point, joining, spread, dw_out, branch_out, slope, grad_dw, joined, sorted_rows, dgrad,
     grads, sems) = refs[3:]
    plane, strip, chip, core = whereabouts()
    slots, active_count = slots_of(mask_ref, branches)

    copies = []

    def fetch(source, target):
        copy = pltpu.make_async_copy(source, target, sems.at[len(copies)])
        copy.start()
        copies.append(copy)

    for hop in range(GROUP):
        fetch(piece_refs[hop], pieces.at[strip ^ hop])
    for place, ref in enumerate(halo_refs):
        fetch(ref, halo_pieces.at[place])
    for hop in range(branches):
        fetch(depth_refs[hop].at[0], depth.at[plane ^ hop])
    early = len(copies)
    fetch(point_ref.at[0], point.at[plane])
    fetch(joining_ref, joining.at[plane])
    half_point, half_join = chans // 2, width // 2
    for hop in range(1, branches):
        for side, ref in ((core, mine_refs[hop - 1]), (1 - core, other_refs[hop - 1])):
            at_point = pl.multiple_of(side * half_point, half_point)
            at_join = pl.multiple_of(side * half_join, half_join)
            fetch(ref.at[pl.ds(0, half_point)], point.at[plane ^ hop, pl.ds(at_point, half_point)])
            fetch(ref.at[pl.ds(half_point, half_join)], joining.at[plane ^ hop, pl.ds(at_join, half_join)])

    for group in range(plan.lanes):
        edge = jnp.zeros((plan.window, plan.pad, 128), f32)
        spread[group, 0:plan.window, 0:plan.pad] = edge
        spread[group, 0:plan.window, plan.pad + plan.sub_rows:plan.tall] = edge
        spread[group, plan.window] = jnp.zeros((plan.tall, 128), f32)
    grads[...] = jnp.zeros_like(grads)
    joined[...] = jnp.zeros_like(joined)
    for copy in copies[:early]:
        copy.wait()

    low_rows = iota((8, 128), 0) < 4

    def lay(source, place, row):
        @pl.loop(0, plan.piece // 16)
        def _(quad):
            at = pl.multiple_of(quad * 16, 16)
            for group in range(plan.lanes):
                lanes = pl.ds(group * 128, 128)
                upper = source[place, pl.ds(at, 16), lanes].astype(f32)
                lower = source[place + 1, pl.ds(at, 16), lanes].astype(f32)
                for part in range(2):
                    a, b = upper[8 * part:8 * part + 8], lower[8 * part:8 * part + 8]
                    column = quad * 4 + 2 * part
                    spread[group, column, row:row + 8] = jnp.where(low_rows, a, pltpu.roll(b, 4, 0))
                    spread[group, column + 1, row:row + 8] = jnp.where(low_rows, pltpu.roll(a, 4, 0), b)

    for pair in range(CHIPS):
        lay(pieces, 2 * pair, plan.pad + 8 * pair)
    if halo:
        for pair in range(2):
            lay(halo_pieces.at[0], 2 * pair, plan.pad - 16 + 8 * pair)
            lay(halo_pieces.at[1], 2 * pair, plan.pad + plan.sub_rows + 8 * pair)

    segments = plan.segments(plane * CHIPS + chip)

    for branch in range(branches):
        @pl.when(mask_ref[branch] > 0)
        def _():
            taps = depth[branch].astype(f32)
            for group in range(plan.lanes):
                kernel = [
                    jnp.broadcast_to(taps[tap:tap + 1, group * 128:(group + 1) * 128], (plan.sub_rows, 128))
                    for tap in range(9)
                ]

                @pl.loop(0, plan.work)
                def _(w):
                    total = None
                    for j in range(3):
                        column = plan.neighbour(segments, w, (j - 1) * (branch + 1))
                        for i in range(3):
                            row = plan.pad + (i - 1) * plan.step_rows * (branch + 1)
                            term = spread[group, column, row:row + plan.sub_rows] * kernel[3 * i + j]
                            total = term if total is None else total + term
                    at = pl.multiple_of(w * plan.sub_rows, plan.sub_rows)
                    dw_out[branch, pl.ds(at, plan.sub_rows), group * 128:(group + 1) * 128] = total.astype(bf16)

    for copy in copies[early:]:
        copy.wait()

    @pl.loop(0, branches)
    def _(branch):
        @pl.when(mask_ref[branch] > 0)
        def _():
            value, derivative = gelu_both(dot(dw_out[branch], point[branch]))
            value = value.astype(bf16)
            branch_out[branch] = value
            slope[branch] = derivative
            joined[...] += dot(value, joining[branch])

    pixel = iota((plan.pixels, 128), 0)
    column, row = pixel // plan.sub_rows, pixel % plan.sub_rows
    source = (row // 2) * plan.tile + 2 * column + row % 2
    lane = iota(source.shape, 1)
    order = jnp.concatenate([one_hot(source == lane + 128 * k) for k in range(plan.pixels // 128)], 1)
    pixel = iota((plan.pixels, plan.pixels), 1)
    column, row = pixel // plan.sub_rows, pixel % plan.sub_rows
    source = (row // 2) * plan.tile + 2 * column + row % 2
    back = one_hot(source == iota(source.shape, 0))
    for pair in range(GROUP):
        for couple in range(branches // 2):
            left = cotangent_ref[pair * branches + 2 * couple].astype(f32)
            right = cotangent_ref[pair * branches + 2 * couple + 1].astype(f32)
            first, second = swap_halves(left, right)
            lanes = pl.ds(couple * 128, 128)
            sorted_rows[pl.ds(2 * pair * plan.tile, plan.tile), lanes] = first
            sorted_rows[pl.ds((2 * pair + 1) * plan.tile, plan.tile), lanes] = second
    cotangent = dot(order, sorted_rows[...].astype(bf16))
    value, derivative = gelu_both(joined[...])
    grad_joined = (cotangent * derivative).astype(bf16)
    sorted_rows[...] = dot(back, value.astype(bf16))
    for pair in range(GROUP):
        for couple in range(branches // 2):
            lanes = pl.ds(couple * 128, 128)
            left = sorted_rows[pl.ds(2 * pair * plan.tile, plan.tile), lanes]
            right = sorted_rows[pl.ds((2 * pair + 1) * plan.tile, plan.tile), lanes]
            first, second = swap_halves(left, right)
            output_ref[pair * branches + 2 * couple] = first.astype(bf16)
            output_ref[pair * branches + 2 * couple + 1] = second.astype(bf16)

    for branch in range(branches):
        slot = slots[branch]

        @pl.when(mask_ref[branch] > 0)
        def _():
            at = pl.multiple_of(slot * plan.grad_rows, 32)
            joining_part = (dot(branch_out[branch], grad_joined, ((0,), (0,))) * scale).astype(bf16)
            for chunk in range(GROUP):
                grads[chunk, pl.ds(at, plan.join_rows)] = joining_part[chunk * plan.join_rows:(chunk + 1) * plan.join_rows]
            grad_branch = dot(grad_joined, joining[branch], ((1,), (1,)))
            grad_pre = (grad_branch * slope[branch]).astype(bf16)
            at = pl.multiple_of(slot * plan.grad_rows + plan.join_rows, 32)
            point_part = (dot(dw_out[branch], grad_pre, ((0,), (0,))) * scale).astype(bf16)
            for chunk in range(GROUP):
                grads[chunk, pl.ds(at, plan.point_rows)] = point_part[
                    chunk * plan.point_rows:(chunk + 1) * plan.point_rows
                ]
            for group in range(plan.lanes):
                grad_dw[group] = dot(grad_pre, point[branch, group * 128:(group + 1) * 128], ((1,), (1,)))
            for group in range(plan.lanes):
                def add_column(w, sums):
                    at = pl.multiple_of(w * plan.sub_rows, plan.sub_rows)
                    given = grad_dw[group, pl.ds(at, plan.sub_rows)]
                    sums = list(sums)
                    for j in range(3):
                        column = plan.neighbour(segments, w, (j - 1) * (branch + 1))
                        for i in range(3):
                            row = plan.pad + (i - 1) * plan.step_rows * (branch + 1)
                            product = spread[group, column, row:row + plan.sub_rows] * given
                            for part in range(plan.sub_rows // 8):
                                sums[3 * i + j] = sums[3 * i + j] + product[8 * part:8 * part + 8]
                    return tuple(sums)

                sums = lax.fori_loop(0, plan.work, add_column, (jnp.zeros((8, 128), f32),) * 9)
                for tap in range(9):
                    dgrad[tap:tap + 1] = jnp.sum(sums[tap], axis=0, keepdims=True) * scale
                lanes = pl.ds(pl.multiple_of((slot % 2) * 128, 128), 128)
                grads[(slot // 2) * CHIPS + group, SLOTS * plan.grad_rows:, lanes] = dgrad[...].astype(bf16)

    half = GROUP // 2
    first = pltpu.make_async_copy(grads.at[pl.ds((1 - core) * half, half)], send_ref, sems.at[0])
    second = pltpu.make_async_copy(grads.at[pl.ds(core * half, half)], keep_ref, sems.at[1])
    first.start()
    second.start()
    first.wait()
    second.wait()


def main_step(plan, scale, mask, cotangent, pieces, halos, depths, point, joining, mine, others):
    halo = len(halos) > 0
    message = SLOTS * plan.grad_rows + 16
    operands = [mask, cotangent, *pieces, *halos, *depths, point, joining, *mine, *others]
    return pl.pallas_call(
        functools.partial(main_kernel, plan, scale, halo),
        out_shape=[
            jax.ShapeDtypeStruct(cotangent.shape, bf16),
            jax.ShapeDtypeStruct((GROUP // 2, message, plan.width), bf16),
            jax.ShapeDtypeStruct((GROUP // 2, message, plan.width), bf16),
        ],
        in_specs=[SMEM, VMEM] + [ANY] * (len(operands) - 2),
        out_specs=[VMEM, ANY, ANY],
        scratch_shapes=[
            pltpu.VMEM((GROUP, plan.piece, plan.chans), bf16),
            pltpu.VMEM((2, 4, plan.piece, plan.chans) if halo else (16, 128), bf16),
            pltpu.VMEM((plan.branches, 9, plan.chans), bf16),
            pltpu.VMEM((plan.branches, plan.chans, plan.width), bf16),
            pltpu.VMEM((plan.branches, plan.width, plan.width), bf16),
            pltpu.VMEM((plan.lanes, plan.window + 1, plan.tall, 128), f32),
            pltpu.VMEM((plan.branches, plan.pixels, plan.chans), bf16),
            pltpu.VMEM((plan.branches, plan.pixels, plan.width), bf16),
            pltpu.VMEM((plan.branches, plan.pixels, plan.width), f32),
            pltpu.VMEM((plan.lanes, plan.pixels, 128), f32),
            pltpu.VMEM((plan.pixels, plan.width), f32),
            pltpu.VMEM((plan.pixels, plan.width), f32),
            pltpu.VMEM((16, 128), f32),
            pltpu.VMEM((GROUP, message, plan.width), bf16),
            pltpu.SemaphoreType.DMA((40,)),
        ],
        compiler_params=pltpu.CompilerParams(vmem_limit_bytes=48 << 20),
        name="forward_and_backward",
    )(*operands)


def chip_sum_kernel(keep_ref, other_ref, *out_refs):
    _, _, chip, _ = whereabouts()
    for hop in range(CHIPS):
        out_refs[hop][...] = (keep_ref[chip ^ hop].astype(f32) + other_ref[chip ^ hop].astype(f32)).astype(bf16)


def chip_sum(keep, other):
    return pl.pallas_call(
        chip_sum_kernel,
        out_shape=[jax.ShapeDtypeStruct(keep.shape[1:], bf16)] * CHIPS,
        in_specs=[VMEM] * 2,
        out_specs=[VMEM] * CHIPS,
        compiler_params=pltpu.CompilerParams(vmem_limit_bytes=40 << 20),
        name="chip_sum",
    )(keep, other)


def plane_sum_kernel(plan, mask_ref, *refs):
    total, out_refs = refs[-1], refs[CHIPS:-1]
    plane, _, _, _ = whereabouts()
    slots, _ = slots_of(mask_ref, plan.branches)
    added = refs[0][...].astype(f32)
    for ref in refs[1:CHIPS]:
        added = added + ref[...].astype(f32)
    total[...] = added
    rows = plan.grad_rows
    for hop in range(plan.branches):
        at = pl.multiple_of(pick(slots, plane ^ hop) * rows, 32)
        out_refs[hop][0:rows] = total[pl.ds(at, rows)].astype(bf16)
        out_refs[hop][rows:rows + 16] = total[SLOTS * rows:].astype(bf16)


def plane_sum(plan, mask, parts):
    return pl.pallas_call(
        functools.partial(plane_sum_kernel, plan),
        out_shape=[jax.ShapeDtypeStruct((plan.grad_rows + 16, plan.width), bf16)] * plan.branches,
        in_specs=[SMEM] + [VMEM] * CHIPS,
        out_specs=[VMEM] * plan.branches,
        scratch_shapes=[pltpu.VMEM(parts[0].shape, f32)],
        compiler_params=pltpu.CompilerParams(vmem_limit_bytes=40 << 20),
        name="plane_sum",
    )(mask, *parts)


def place_grads_kernel(plan, mask_ref, chunks_ref, joining_ref, point_ref, depth_ref):
    plane, _, _, _ = whereabouts()
    slots, _ = slots_of(mask_ref, plan.branches)
    slot = pick(slots, plane)
    active = pick([mask_ref[branch] for branch in range(plan.branches)], plane) > 0
    rows = plan.grad_rows
    for chip in range(CHIPS):
        for core in range(2):
            chunk = jnp.where(active, chunks_ref[2 * chip + core, 0:rows].astype(f32), 0.0)
            at = core * CHIPS + chip
            joining_ref[at * plan.join_rows:(at + 1) * plan.join_rows] = chunk[:plan.join_rows]
            point_ref[0, at * plan.point_rows:(at + 1) * plan.point_rows] = chunk[plan.join_rows:]
        lanes = pl.ds(pl.multiple_of((slot % 2) * 128, 128), 128)
        part = chunks_ref[2 * chip + slot // 2, rows:rows + 16, lanes].astype(f32)
        depth_ref[0, :, chip * 128:(chip + 1) * 128] = jnp.where(active, part, 0.0)[0:9]


def place_grads(plan, mask, chunks):
    return pl.pallas_call(
        functools.partial(place_grads_kernel, plan),
        out_shape=[
            jax.ShapeDtypeStruct((plan.width, plan.width), f32),
            jax.ShapeDtypeStruct((1, plan.chans, plan.width), f32),
            jax.ShapeDtypeStruct((1, 9, plan.chans), f32),
        ],
        in_specs=[SMEM, VMEM],
        out_specs=[VMEM] * 3,
        compiler_params=pltpu.CompilerParams(vmem_limit_bytes=40 << 20),
        name="place_grads",
    )(mask, chunks)


def per_device(features, cotangent, depth_weight, point_weight, joining_weight, branch_mask):
    row_count, col_count, chan_count = features.shape
    strips = lax.axis_size("strip")
    branches = lax.axis_size("branch")
    width = joining_weight.shape[1]
    plan = Plan(row_count, col_count, chan_count, width, branches)
    scale = 1.0 / math.sqrt(row_count * col_count * strips)
    groups = None if strips == GROUP else [list(range(g, g + GROUP)) for g in range(0, strips, GROUP)]
    core = lax.axis_index("strip") % 2

    def flip_strip(value, hop):
        return lax.ppermute(value, "strip", [(s, s ^ hop) for s in range(strips)])

    def flip_branch(value, hop):
        return lax.ppermute(value, "branch", [(b, b ^ hop) for b in range(branches)])

    def all_to_all(tiles):
        if groups is None:
            return lax.all_to_all(tiles, ("strip", "branch"), 0, 0, tiled=True)
        tiles = tiles.reshape(GROUP, branches, *tiles.shape[1:])
        tiles = lax.all_to_all(tiles, "branch", 1, 1, tiled=True)
        tiles = lax.all_to_all(tiles, "strip", 0, 0, tiled=True, axis_index_groups=groups)
        return tiles.reshape(GROUP * branches, *tiles.shape[2:])

    depths = [depth_weight] + [flip_branch(depth_weight, hop) for hop in range(1, branches)]
    half = jnp.concatenate([
        lax.dynamic_slice(point_weight[0], (core * (chan_count // 2), 0), (chan_count // 2, width)),
        lax.dynamic_slice(joining_weight, (core * (width // 2), 0), (width // 2, width)),
    ])
    mine = [flip_branch(half, hop) for hop in range(1, branches)]
    others = [flip_strip(value, 1) for value in mine]

    sent = spread_features(plan, features)
    pieces = [sent[0]] + [flip_strip(sent[hop], hop) for hop in range(1, GROUP)]
    halos = []
    if groups is not None:
        strip = lax.axis_index("strip") % GROUP
        stacked = jnp.take(jnp.stack(pieces), jnp.arange(GROUP) ^ strip, axis=0)
        down = [(s, s + GROUP) for s in range(strips - GROUP)]
        up = [(s + GROUP, s) for s in range(strips - GROUP)]
        halos = [lax.ppermute(stacked[GROUP - 4:], "strip", down), lax.ppermute(stacked[:4], "strip", up)]

    cotangent_tiles = all_to_all(send_cotangent(plan, cotangent))
    output_tiles, keep, send = main_step(
        plan, scale, branch_mask, cotangent_tiles, pieces, halos, depths, point_weight, joining_weight, mine, others
    )
    parts = chip_sum(keep, flip_strip(send, 1))
    parts = [parts[0]] + [flip_strip(parts[hop], 2 * hop) for hop in range(1, CHIPS)]
    output = place_output(plan, all_to_all(output_tiles))
    shares = plane_sum(plan, branch_mask, parts)
    shares = [shares[0]] + [flip_branch(shares[hop], hop) for hop in range(1, branches)]
    share = sum(value.astype(f32) for value in shares)
    if groups is not None:
        peers = [list(range(s, strips, GROUP)) for s in range(GROUP)]
        share = lax.psum(share, "strip", axis_index_groups=peers)
    chunks = lax.all_gather(share.astype(bf16), "strip", axis=0, axis_index_groups=groups)
    joining_total, point_total, depth_total = place_grads(plan, branch_mask, chunks)
    return (output, joining_total, point_total, depth_total)


def solution(mesh):
    placed = (
        P("strip", None, None),
        P("strip", None, "branch"),
        P("branch", None, None),
        P("branch", None, None),
        P("branch", None),
        P(),
    )
    return jax.shard_map(
        per_device,
        mesh=mesh,
        in_specs=placed,
        out_specs=(
            P("strip", None, "branch"),
            P("branch", None),
            P("branch", None, None),
            P("branch", None, None),
        ),
        check_vma=False,
    )
```

```python
import functools
import math

import jax
import jax.numpy as jnp
from jax import lax
from jax.experimental import pallas as pl
from jax.experimental.pallas import tpu as pltpu
from jax.sharding import PartitionSpec as P

DILATION_STEP = 6
GROUP = 8
CHIPS = 4
SLOTS = 3

tanh_coef = 0.7978845608
cubic_coef = 0.044715
slope_coef = 0.134145

f32, bf16, i32 = jnp.float32, jnp.bfloat16, jnp.int32
VMEM = pl.BlockSpec(memory_space=pltpu.VMEM)
SMEM = pl.BlockSpec(memory_space=pltpu.SMEM)
ANY = pl.BlockSpec(memory_space=pl.ANY)
HBM = pl.BlockSpec(memory_space=pltpu.HBM)


def gelu_both(values):
    square = values * values
    inner = jnp.tanh(tanh_coef * (values + cubic_coef * values * square))
    half = 0.5 * (1.0 + inner)
    slope = half + 0.5 * values * (1.0 - inner * inner) * tanh_coef * (1.0 + slope_coef * square)
    return values * half, slope


def dot(left, right, dims=((1,), (0,))):
    return lax.dot_general(left, right, (dims, ((), ())), preferred_element_type=f32)


def iota(shape, dim):
    return lax.broadcasted_iota(i32, shape, dim)


def one_hot(mask):
    return jnp.where(mask, 1.0, 0.0).astype(bf16)


class Plan:
    def __init__(self, row_count, col_count, chan_count, width, branches):
        self.rows, self.cols, self.chans, self.width, self.branches = row_count, col_count, chan_count, width, branches
        self.classes = DILATION_STEP
        self.run = col_count // DILATION_STEP
        self.work = col_count // (branches * CHIPS)
        self.taps_t = row_count // 2
        self.sub_rows = GROUP * self.taps_t
        self.pixels = self.sub_rows * self.work
        self.lanes = chan_count // 128
        self.window = max(self.segments(m)[5] for m in range(branches * CHIPS))
        self.piece = self.window * self.taps_t
        self.part = width // branches
        self.step_rows = DILATION_STEP // 2
        self.pad = -(-self.step_rows * branches // 16) * 16
        self.tall = self.pad + self.sub_rows + self.pad
        self.grad_rows = (width + chan_count) // GROUP
        self.join_rows = width // GROUP
        self.point_rows = chan_count // GROUP
        self.tile = 2 * self.work
        self.depth_rows = -(-9 * self.lanes // GROUP // 8) * 8
        self.wide = -(-self.cols // 128) * 128

    def segments(self, m):
        smaller, larger = (min, max) if isinstance(m, int) else (jnp.minimum, jnp.maximum)
        first = m * self.work
        klass = first // self.run
        start = first - klass * self.run
        length = smaller(self.work, self.run - start)
        low = larger(0, start - self.branches)
        size = smaller(self.run, start + length + self.branches) - low
        rest = self.work - length
        if isinstance(m, int):
            total = size + (min(self.run, rest + self.branches) if rest else 0)
        else:
            total = size + jnp.where(rest > 0, jnp.minimum(self.run, rest + self.branches), 0)
        return klass, start, length, low, size, total

    def column(self, m, w):
        klass, start, length, _, _, _ = self.segments(m)
        return jnp.where(w < length, self.classes * (start + w) + klass, self.classes * (w - length) + klass + 1)

    def window_column(self, m, j):
        klass, _, _, low, size, total = self.segments(m)
        inside = jnp.where(j < size, self.classes * (low + j) + klass, self.classes * (j - size) + klass + 1)
        return jnp.where(j < total, inside, -(1 << 20))

    def neighbour(self, segments, w, shift):
        _, start, length, low, size, _ = segments
        first = w < length
        place = jnp.where(first, start + w, w - length) + shift
        found = jnp.where(first, place - low, size + place)
        return jnp.where(jnp.logical_and(place >= 0, place < self.run), found, self.window)


def whereabouts():
    strip = lax.axis_index("strip") % GROUP
    return lax.axis_index("branch"), strip, strip // 2, strip % 2


def slots_of(mask_ref, branches):
    slots, count = [], 0
    for branch in range(branches):
        slots.append(jnp.minimum(count, SLOTS - 1) + 0 * mask_ref[branch])
        count = count + mask_ref[branch]
    return slots, count


def pick(values, index):
    result = values[0]
    for place in range(1, len(values)):
        result = jnp.where(index == place, values[place], result)
    return result


def tile_selector(plan):
    blocks = []
    for chip in range(CHIPS):
        for plane in range(plan.branches):
            row = iota((plan.tile, 128), 0)
            column = plan.column(plane * CHIPS + chip, row // 2)
            blocks.append(column + (row % 2) * plan.wide)
    target = jnp.concatenate(blocks, 0)
    lane = iota(target.shape, 1)
    return jnp.concatenate([one_hot(target == lane + 128 * k) for k in range(2 * plan.wide // 128)], 1)


def halve_kernel(plan, point_ref, joining_ref, half_ref, sems):
    _, _, _, core = whereabouts()
    half_point, half_join = plan.chans // 2, plan.width // 2
    copies = [
        pltpu.make_async_copy(
            point_ref.at[0, pl.ds(pl.multiple_of(core * half_point, half_point), half_point)],
            half_ref.at[pl.ds(0, half_point)],
            sems.at[0],
        ),
        pltpu.make_async_copy(
            joining_ref.at[pl.ds(pl.multiple_of(core * half_join, half_join), half_join)],
            half_ref.at[pl.ds(half_point, half_join)],
            sems.at[1],
        ),
    ]
    for copy in copies:
        copy.start()
    for copy in copies:
        copy.wait()


def halve_weights(plan, point, joining):
    return pl.pallas_call(
        functools.partial(halve_kernel, plan),
        out_shape=jax.ShapeDtypeStruct(((plan.chans + plan.width) // 2, plan.width), bf16),
        in_specs=[HBM] * 2,
        out_specs=VMEM,
        scratch_shapes=[pltpu.SemaphoreType.DMA((2,))],
        compiler_params=pltpu.CompilerParams(vmem_limit_bytes=8 << 20),
        name="halve_weights",
    )(point, joining)


def spread_kernel(plan, features_ref, keep_ref, send_ref):
    plane, _, _, core = whereabouts()
    depth = plan.taps_t * plan.cols
    targets = []
    for chip in range(CHIPS):
        row = iota((plan.piece, 128), 0)
        column = plan.window_column(plane * CHIPS + chip, row // plan.taps_t)
        targets.append(column + (row % plan.taps_t) * plan.cols)
    target = jnp.concatenate(targets, 0)
    lane = iota(target.shape, 1)
    chosen = jnp.concatenate([one_hot(target == lane + 128 * k) for k in range(depth // 128)], 1)
    for flip, out_ref in enumerate((keep_ref, send_ref)):
        rows = jnp.concatenate([features_ref[2 * t + (core ^ flip)] for t in range(plan.taps_t)], 0)
        found = dot(chosen, rows).astype(bf16)
        for chip in range(CHIPS):
            out_ref[chip] = found[chip * plan.piece:(chip + 1) * plan.piece]


def spread_features(plan, features):
    half = jax.ShapeDtypeStruct((CHIPS, plan.piece, plan.chans), bf16)
    return pl.pallas_call(
        functools.partial(spread_kernel, plan),
        out_shape=[half, half],
        in_specs=[VMEM],
        out_specs=[VMEM] * 2,
        compiler_params=pltpu.CompilerParams(vmem_limit_bytes=16 << 20),
        name="spread_features",
    )(features)


def join_kernel(plan, keep_ref, other_ref, *out_refs):
    _, _, chip, _ = whereabouts()
    for hop in range(CHIPS):
        out_refs[hop][0:plan.piece] = keep_ref[chip ^ hop]
        out_refs[hop][plan.piece:] = other_ref[chip ^ hop]


def join_features(plan, keep, other):
    return pl.pallas_call(
        functools.partial(join_kernel, plan),
        out_shape=[jax.ShapeDtypeStruct((2 * plan.piece, plan.chans), bf16)] * CHIPS,
        in_specs=[VMEM] * 2,
        out_specs=[VMEM] * CHIPS,
        compiler_params=pltpu.CompilerParams(vmem_limit_bytes=8 << 20),
        name="join_features",
    )(keep, other)


def send_cotangent_kernel(plan, cotangent_ref, depth_ref, tiles_ref, cotangent, depth, taps, sems):
    _, strip, _, _ = whereabouts()
    copies = [
        pltpu.make_async_copy(cotangent_ref, cotangent, sems.at[0]),
        pltpu.make_async_copy(depth_ref, depth, sems.at[1]),
    ]
    for copy in copies:
        copy.start()
    chosen = tile_selector(plan)
    for copy in copies:
        copy.wait()

    taps[...] = jnp.zeros_like(taps)
    values = depth[0].astype(f32)
    for tap in range(9):
        for group in range(plan.lanes):
            row = tap * plan.lanes + group
            taps[row:row + 1] = values[tap:tap + 1, group * 128:(group + 1) * 128]
    share = taps[pl.ds(pl.multiple_of(strip * plan.depth_rows, 8), plan.depth_rows)]
    fill = jnp.zeros((plan.part, plan.wide - plan.cols), f32)
    blocks = []
    for parity in range(2):
        for high in range(2):
            rows = []
            for low in range(2):
                rows += [cotangent[2 * (2 * high + low) + parity].astype(f32), fill]
            blocks.append(jnp.concatenate(rows, 1))
    found = dot(chosen, jnp.concatenate(blocks, 0).astype(bf16), ((1,), (1,)))
    for chip in range(CHIPS):
        for parity in range(2):
            for plane in range(plan.branches):
                at = (chip * plan.branches + plane) * plan.tile
                tile = found[at:at + plan.tile, parity * 128:(parity + 1) * 128]
                tiles_ref[(2 * chip + parity) * plan.branches + plane] = jnp.concatenate([tile, share], 0).astype(bf16)


def send_cotangent(plan, cotangent, depth):
    return pl.pallas_call(
        functools.partial(send_cotangent_kernel, plan),
        out_shape=jax.ShapeDtypeStruct((GROUP * plan.branches, plan.tile + plan.depth_rows, 128), bf16),
        in_specs=[HBM] * 2,
        out_specs=VMEM,
        scratch_shapes=[
            pltpu.VMEM(cotangent.shape, bf16),
            pltpu.VMEM(depth.shape, bf16),
            pltpu.VMEM((GROUP * plan.depth_rows, 128), f32),
            pltpu.SemaphoreType.DMA((2,)),
        ],
        compiler_params=pltpu.CompilerParams(vmem_limit_bytes=16 << 20),
        cost_estimate=pl.CostEstimate(flops=1, bytes_accessed=1, transcendentals=0),
        name="send_cotangent",
    )(cotangent, depth)


def place_output_kernel(plan, tiles_ref, out_ref):
    chosen = tile_selector(plan)
    halves = []
    for parity in range(2):
        blocks = []
        for chip in range(CHIPS):
            for plane in range(plan.branches):
                blocks.append(tiles_ref[(2 * chip + parity) * plan.branches + plane].astype(f32))
        halves.append(jnp.concatenate(blocks, 0))
    found = dot(jnp.concatenate(halves, 1).astype(bf16), chosen, ((0,), (0,))).astype(bf16)
    for parity in range(2):
        for high in range(2):
            for low in range(2):
                at = parity * 128 + high * plan.part
                out_ref[2 * (2 * high + low) + parity] = found[
                    at:at + plan.part, low * plan.wide:low * plan.wide + plan.cols
                ]


def place_output(plan, tiles):
    return pl.pallas_call(
        functools.partial(place_output_kernel, plan),
        out_shape=jax.ShapeDtypeStruct((plan.rows, plan.part, plan.cols), bf16),
        in_specs=[VMEM],
        out_specs=VMEM,
        compiler_params=pltpu.CompilerParams(vmem_limit_bytes=16 << 20),
        name="place_output",
    )(tiles)


def swap_halves(left, right):
    low = iota(left.shape, 1) < 64
    return (
        jnp.where(low, left, pltpu.roll(right, 64, 1)),
        jnp.where(low, pltpu.roll(left, 64, 1), right),
    )


def main_kernel(plan, scale, halo, mask_ref, cotangent_ref, *refs):
    branches, width, chans = plan.branches, plan.width, plan.chans
    piece_refs, refs = refs[:CHIPS], refs[CHIPS:]
    halo_refs, refs = (refs[:2], refs[2:]) if halo else ((), refs)
    (point_ref, joining_ref), refs = refs[:2], refs[2:]
    mine_refs, refs = refs[:branches - 1], refs[branches - 1:]
    other_refs, refs = refs[:branches - 1], refs[branches - 1:]
    output_ref, keep_ref, send_ref, grad_pre_ref, point, spread = refs[:6]
    pieces, halo_pieces, dw_out, joining, branch_out, slope, joined, sorted_rows, grads, sems = refs[6:]
    plane, strip, chip, core = whereabouts()
    slots, _ = slots_of(mask_ref, branches)

    copies = []

    def fetch(source, target):
        copy = pltpu.make_async_copy(source, target, sems.at[len(copies)])
        copy.start()
        copies.append(copy)

    for hop in range(CHIPS):
        for flip in range(2):
            fetch(
                piece_refs[hop].at[pl.ds(flip * plan.piece, plan.piece)], pieces.at[2 * (chip ^ hop) + (core ^ flip)]
            )
    for place, ref in enumerate(halo_refs):
        fetch(ref, halo_pieces.at[place])
    early = len(copies)
    fetch(point_ref.at[0], point.at[plane])
    fetch(joining_ref, joining.at[plane])
    half_point, half_join = chans // 2, width // 2
    for hop in range(1, branches):
        for side, ref in ((core, mine_refs[hop - 1]), (1 - core, other_refs[hop - 1])):
            at_point = pl.multiple_of(side * half_point, half_point)
            at_join = pl.multiple_of(side * half_join, half_join)
            fetch(ref.at[pl.ds(0, half_point)], point.at[plane ^ hop, pl.ds(at_point, half_point)])
            fetch(ref.at[pl.ds(half_point, half_join)], joining.at[plane ^ hop, pl.ds(at_join, half_join)])

    for group in range(plan.lanes):
        edge = jnp.zeros((plan.window, plan.pad, 128), f32)
        spread[group, 0:plan.window, 0:plan.pad] = edge
        spread[group, 0:plan.window, plan.pad + plan.sub_rows:plan.tall] = edge
        spread[group, plan.window] = jnp.zeros((plan.tall, 128), f32)

    low_rows = iota((8, 128), 0) < 4

    def lay(source, place, row):
        @pl.loop(0, plan.piece // 16)
        def _(quad):
            at = pl.multiple_of(quad * 16, 16)
            for group in range(plan.lanes):
                lanes = pl.ds(group * 128, 128)
                upper = source[place, pl.ds(at, 16), lanes].astype(f32)
                lower = source[place + 1, pl.ds(at, 16), lanes].astype(f32)
                for part in range(2):
                    a, b = upper[8 * part:8 * part + 8], lower[8 * part:8 * part + 8]
                    column = quad * 4 + 2 * part
                    spread[group, column, row:row + 8] = jnp.where(low_rows, a, pltpu.roll(b, 4, 0))
                    spread[group, column + 1, row:row + 8] = jnp.where(low_rows, pltpu.roll(a, 4, 0), b)

    for copy in copies[:early]:
        copy.wait()
    for pair in range(CHIPS):
        lay(pieces, 2 * pair, plan.pad + 8 * pair)
    if halo:
        for pair in range(2):
            lay(halo_pieces.at[0], 2 * pair, plan.pad - 16 + 8 * pair)
            lay(halo_pieces.at[1], 2 * pair, plan.pad + plan.sub_rows + 8 * pair)

    segments = plan.segments(plane * CHIPS + chip)
    for branch in range(plan.branches):
        @pl.when(mask_ref[branch] > 0)
        def _():
            shares = [
                cotangent_ref[strip * plan.branches + branch].astype(f32)
                for strip in range(-(-9 * plan.lanes // plan.depth_rows))
            ]
            for group in range(plan.lanes):
                kernel = []
                for tap in range(9):
                    row = tap * plan.lanes + group
                    at = plan.tile + row % plan.depth_rows
                    kernel.append(jnp.broadcast_to(shares[row // plan.depth_rows][at:at + 1], (plan.sub_rows, 128)))

                @pl.loop(0, plan.work)
                def _(w):
                    total = None
                    for j in range(3):
                        column = plan.neighbour(segments, w, (j - 1) * (branch + 1))
                        for i in range(3):
                            row = plan.pad + (i - 1) * plan.step_rows * (branch + 1)
                            term = spread[group, column, row:row + plan.sub_rows] * kernel[3 * i + j]
                            total = term if total is None else total + term
                    at = pl.multiple_of(w * plan.sub_rows, plan.sub_rows)
                    dw_out[branch, pl.ds(at, plan.sub_rows), group * 128:(group + 1) * 128] = total.astype(bf16)

    pixel = iota((plan.pixels, 128), 0)
    column, row = pixel // plan.sub_rows, pixel % plan.sub_rows
    source = (row // 2) * plan.tile + 2 * column + row % 2
    lane = iota(source.shape, 1)
    order = jnp.concatenate([one_hot(source == lane + 128 * k) for k in range(plan.pixels // 128)], 1)
    for pair in range(GROUP):
        for couple in range(branches // 2):
            left = cotangent_ref[pair * branches + 2 * couple].astype(f32)[:plan.tile]
            right = cotangent_ref[pair * branches + 2 * couple + 1].astype(f32)[:plan.tile]
            first, second = swap_halves(left, right)
            lanes = pl.ds(couple * 128, 128)
            sorted_rows[pl.ds(2 * pair * plan.tile, plan.tile), lanes] = first
            sorted_rows[pl.ds((2 * pair + 1) * plan.tile, plan.tile), lanes] = second
    cotangent = dot(order, sorted_rows[...].astype(bf16))
    joined[...] = jnp.zeros_like(joined)
    grads[...] = jnp.zeros_like(grads)
    for copy in copies[early:]:
        copy.wait()

    @pl.loop(0, branches)
    def _(branch):
        @pl.when(mask_ref[branch] > 0)
        def _():
            value, derivative = gelu_both(dot(dw_out[branch], point[branch]))
            value = value.astype(bf16)
            branch_out[branch] = value
            slope[branch] = derivative
            joined[...] += dot(value, joining[branch])

    value, derivative = gelu_both(joined[...])
    grad_joined = (cotangent * derivative).astype(bf16)
    pixel = iota((plan.pixels, plan.pixels), 1)
    column, row = pixel // plan.sub_rows, pixel % plan.sub_rows
    source = (row // 2) * plan.tile + 2 * column + row % 2
    back = one_hot(source == iota(source.shape, 0))
    sorted_rows[...] = dot(back, value.astype(bf16))
    for pair in range(GROUP):
        for couple in range(branches // 2):
            lanes = pl.ds(couple * 128, 128)
            left = sorted_rows[pl.ds(2 * pair * plan.tile, plan.tile), lanes]
            right = sorted_rows[pl.ds((2 * pair + 1) * plan.tile, plan.tile), lanes]
            first, second = swap_halves(left, right)
            output_ref[pair * branches + 2 * couple] = first.astype(bf16)
            output_ref[pair * branches + 2 * couple + 1] = second.astype(bf16)

    for branch in range(branches):
        slot = slots[branch]

        @pl.when(mask_ref[branch] > 0)
        def _():
            at = pl.multiple_of(slot * plan.grad_rows, 32)
            joining_part = (dot(branch_out[branch], grad_joined, ((0,), (0,))) * scale).astype(bf16)
            for chunk in range(GROUP):
                grads[chunk, pl.ds(at, plan.join_rows)] = joining_part[chunk * plan.join_rows:(chunk + 1) * plan.join_rows]
            grad_branch = dot(grad_joined, joining[branch], ((1,), (1,)))
            grad_pre = (grad_branch * slope[branch]).astype(bf16)
            grad_pre_ref[branch] = grad_pre
            at = pl.multiple_of(slot * plan.grad_rows + plan.join_rows, 32)
            point_part = (dot(dw_out[branch], grad_pre, ((0,), (0,))) * scale).astype(bf16)
            for chunk in range(GROUP):
                grads[chunk, pl.ds(at, plan.point_rows)] = point_part[
                    chunk * plan.point_rows:(chunk + 1) * plan.point_rows
                ]

    half = GROUP // 2
    first = pltpu.make_async_copy(grads.at[pl.ds((1 - core) * half, half)], send_ref, sems.at[0])
    second = pltpu.make_async_copy(grads.at[pl.ds(core * half, half)], keep_ref, sems.at[1])
    first.start()
    second.start()
    first.wait()
    second.wait()


def main_step(plan, scale, mask, tiles, pieces, halos, point, joining, mine, others):
    operands = [mask, tiles, *pieces, *halos, point, joining, *mine, *others]
    half = jax.ShapeDtypeStruct((GROUP // 2, SLOTS * plan.grad_rows, plan.width), bf16)
    return pl.pallas_call(
        functools.partial(main_kernel, plan, scale, len(halos) > 0),
        out_shape=[
            jax.ShapeDtypeStruct((GROUP * plan.branches, plan.tile, 128), bf16),
            half,
            half,
            jax.ShapeDtypeStruct((plan.branches, plan.pixels, plan.width), bf16),
            jax.ShapeDtypeStruct((plan.branches, plan.chans, plan.width), bf16),
            jax.ShapeDtypeStruct((plan.lanes, plan.window + 1, plan.tall, 128), f32),
        ],
        in_specs=[SMEM, VMEM] + [ANY] * (len(operands) - 2),
        out_specs=[VMEM, ANY, ANY, VMEM, VMEM, VMEM],
        scratch_shapes=[
            pltpu.VMEM((GROUP, plan.piece, plan.chans), bf16),
            pltpu.VMEM((2, 4, plan.piece, plan.chans) if halos else (16, 128), bf16),
            pltpu.VMEM((plan.branches, plan.pixels, plan.chans), bf16),
            pltpu.VMEM((plan.branches, plan.width, plan.width), bf16),
            pltpu.VMEM((plan.branches, plan.pixels, plan.width), bf16),
            pltpu.VMEM((plan.branches, plan.pixels, plan.width), f32),
            pltpu.VMEM((plan.pixels, plan.width), f32),
            pltpu.VMEM((plan.pixels, plan.width), f32),
            pltpu.VMEM((GROUP, SLOTS * plan.grad_rows, plan.width), bf16),
            pltpu.SemaphoreType.DMA((GROUP + 2 + 4 * plan.branches,)),
        ],
        compiler_params=pltpu.CompilerParams(vmem_limit_bytes=32 << 20),
        cost_estimate=pl.CostEstimate(flops=1 << 31, bytes_accessed=1 << 24, transcendentals=0),
        name="forward_and_backward",
    )(*operands)


def depth_grad_kernel(plan, scale, mask_ref, grad_pre_ref, point, spread, out_ref, grad_dw, rows):
    plane, _, chip, _ = whereabouts()
    slots, _ = slots_of(mask_ref, plan.branches)
    segments = plan.segments(plane * CHIPS + chip)
    out_ref[...] = jnp.zeros_like(out_ref)
    rows[...] = jnp.zeros_like(rows)
    for branch in range(plan.branches):
        @pl.when(mask_ref[branch] > 0)
        def _():
            grad_pre = grad_pre_ref[branch]
            for group in range(plan.lanes):
                grad_dw[group] = dot(grad_pre, point[branch, group * 128:(group + 1) * 128], ((1,), (1,)))
            for group in range(plan.lanes):
                def add_column(w, sums):
                    at = pl.multiple_of(w * plan.sub_rows, plan.sub_rows)
                    given = grad_dw[group, pl.ds(at, plan.sub_rows)]
                    sums = list(sums)
                    for j in range(3):
                        column = plan.neighbour(segments, w, (j - 1) * (branch + 1))
                        for i in range(3):
                            row = plan.pad + (i - 1) * plan.step_rows * (branch + 1)
                            product = spread[group, column, row:row + plan.sub_rows] * given
                            for part in range(plan.sub_rows // 8):
                                sums[3 * i + j] = sums[3 * i + j] + product[8 * part:8 * part + 8]
                    return tuple(sums)

                sums = lax.fori_loop(0, plan.work, add_column, (jnp.zeros((8, 128), f32),) * 9)
                lanes = slice((group % 2) * 128, (group % 2) * 128 + 128)
                for tap in range(9):
                    row = 2 * tap + group // 2
                    rows[row:row + 1, lanes] = jnp.sum(sums[tap], axis=0, keepdims=True) * scale
            out_ref[slots[branch]] = rows[...].astype(bf16)


def depth_grad(plan, scale, mask, grad_pre, point, spread):
    return pl.pallas_call(
        functools.partial(depth_grad_kernel, plan, scale),
        out_shape=jax.ShapeDtypeStruct((SLOTS, 32, plan.width), bf16),
        in_specs=[SMEM] + [VMEM] * 3,
        out_specs=VMEM,
        scratch_shapes=[
            pltpu.VMEM((plan.lanes, plan.pixels, 128), f32),
            pltpu.VMEM((32, plan.width), f32),
        ],
        compiler_params=pltpu.CompilerParams(vmem_limit_bytes=24 << 20),
        cost_estimate=pl.CostEstimate(flops=1 << 26, bytes_accessed=1 << 24, transcendentals=0),
        name="depth_grad",
    )(mask, grad_pre, point, spread)


def chip_sum_kernel(keep_ref, other_ref, *out_refs):
    _, _, chip, _ = whereabouts()
    for hop in range(CHIPS):
        out_refs[hop][...] = (keep_ref[chip ^ hop].astype(f32) + other_ref[chip ^ hop].astype(f32)).astype(bf16)


def chip_sum(keep, other):
    return pl.pallas_call(
        chip_sum_kernel,
        out_shape=[jax.ShapeDtypeStruct(keep.shape[1:], bf16)] * CHIPS,
        in_specs=[VMEM] * 2,
        out_specs=[VMEM] * CHIPS,
        compiler_params=pltpu.CompilerParams(vmem_limit_bytes=16 << 20),
        name="chip_sum",
    )(keep, other)


def plane_sum_kernel(plan, mask_ref, depth_ref, *refs):
    total, out_refs = refs[-1], refs[CHIPS:-1]
    plane, _, _, _ = whereabouts()
    slots, _ = slots_of(mask_ref, plan.branches)
    added = refs[0][...].astype(f32)
    for ref in refs[1:CHIPS]:
        added = added + ref[...].astype(f32)
    total[...] = added
    rows = plan.grad_rows
    for hop in range(plan.branches):
        slot = pick(slots, plane ^ hop)
        out_refs[hop][0:rows] = total[pl.ds(pl.multiple_of(slot * rows, 32), rows)].astype(bf16)
        out_refs[hop][rows:] = depth_ref[slot]


def plane_sum(plan, mask, depth, parts):
    return pl.pallas_call(
        functools.partial(plane_sum_kernel, plan),
        out_shape=[jax.ShapeDtypeStruct((plan.grad_rows + depth.shape[1], plan.width), bf16)] * plan.branches,
        in_specs=[SMEM] + [VMEM] * (1 + CHIPS),
        out_specs=[VMEM] * plan.branches,
        scratch_shapes=[pltpu.VMEM(parts[0].shape, f32)],
        compiler_params=pltpu.CompilerParams(vmem_limit_bytes=16 << 20),
        name="plane_sum",
    )(mask, depth, *parts)


def place_grads_kernel(plan, mask_ref, chunks_ref, joining_ref, point_ref, depth_ref):
    plane, _, _, _ = whereabouts()
    active = pick([mask_ref[branch] for branch in range(plan.branches)], plane) > 0
    rows = plan.grad_rows
    taps = None
    for chip in range(CHIPS):
        for core in range(2):
            chunk = jnp.where(active, chunks_ref[2 * chip + core].astype(f32), 0.0)
            at = core * CHIPS + chip
            joining_ref[at * plan.join_rows:(at + 1) * plan.join_rows] = chunk[:plan.join_rows]
            point_ref[0, at * plan.point_rows:(at + 1) * plan.point_rows] = chunk[plan.join_rows:rows]
            taps = chunk[rows:] if taps is None else taps + chunk[rows:]
    for tap in range(9):
        for group in range(plan.lanes):
            row, lane = 2 * tap + group // 2, (group % 2) * 128
            depth_ref[0, tap:tap + 1, group * 128:(group + 1) * 128] = taps[row:row + 1, lane:lane + 128]


def place_grads(plan, mask, chunks):
    return pl.pallas_call(
        functools.partial(place_grads_kernel, plan),
        out_shape=[
            jax.ShapeDtypeStruct((plan.width, plan.width), f32),
            jax.ShapeDtypeStruct((1, plan.chans, plan.width), f32),
            jax.ShapeDtypeStruct((1, 9, plan.chans), f32),
        ],
        in_specs=[SMEM, VMEM],
        out_specs=[VMEM] * 3,
        compiler_params=pltpu.CompilerParams(vmem_limit_bytes=16 << 20),
        name="place_grads",
    )(mask, chunks)


def per_device(features, cotangent, depth_weight, point_weight, joining_weight, branch_mask):
    row_count, col_count, chan_count = features.shape
    strips = lax.axis_size("strip")
    branches = lax.axis_size("branch")
    width = joining_weight.shape[1]
    plan = Plan(row_count, col_count, chan_count, width, branches)
    scale = 1.0 / math.sqrt(row_count * col_count * strips)
    groups = None if strips == GROUP else [list(range(g, g + GROUP)) for g in range(0, strips, GROUP)]

    def flip_strip(value, hop):
        return lax.ppermute(value, "strip", [(s, s ^ hop) for s in range(strips)])

    def flip_branch(value, hop):
        return lax.ppermute(value, "branch", [(b, b ^ hop) for b in range(branches)])

    def all_to_all(tiles):
        if groups is None:
            return lax.all_to_all(tiles, ("strip", "branch"), 0, 0, tiled=True)
        tiles = tiles.reshape(GROUP, branches, *tiles.shape[1:])
        tiles = lax.all_to_all(tiles, "branch", 1, 1, tiled=True)
        tiles = lax.all_to_all(tiles, "strip", 0, 0, tiled=True, axis_index_groups=groups)
        return tiles.reshape(GROUP * branches, *tiles.shape[2:])

    half = halve_weights(plan, point_weight, joining_weight)
    mine = [flip_branch(half, hop) for hop in range(1, branches)]

    keep, send = spread_features(plan, features)
    joint = join_features(plan, keep, flip_strip(send, 1))
    pieces = [joint[0]] + [flip_strip(joint[hop], 2 * hop) for hop in range(1, CHIPS)]
    mine, pieces = lax.optimization_barrier((mine, pieces))
    others = [flip_strip(value, 1) for value in mine]
    halos = []
    if groups is not None:
        strip = lax.axis_index("strip") % GROUP
        near = jnp.stack(pieces).reshape(CHIPS, 2, plan.piece, plan.chans)
        at = jnp.arange(GROUP)
        near = near[(at // 2) ^ (strip // 2), (at % 2) ^ (strip % 2)]
        down = [(s, s + GROUP) for s in range(strips - GROUP)]
        up = [(s + GROUP, s) for s in range(strips - GROUP)]
        halos = [lax.ppermute(near[GROUP - 4:], "strip", down), lax.ppermute(near[:4], "strip", up)]
    tiles = all_to_all(send_cotangent(plan, jnp.swapaxes(cotangent, 1, 2), depth_weight))

    output_tiles, keep, send, grad_pre, points, spread = main_step(
        plan, scale, branch_mask, tiles, pieces, halos, point_weight, joining_weight, mine, others
    )
    parts = chip_sum(keep, flip_strip(send, 1))
    parts, output_tiles, grad_pre = lax.optimization_barrier((parts, output_tiles, grad_pre))
    parts = [parts[0]] + [flip_strip(parts[hop], 2 * hop) for hop in range(1, CHIPS)]
    taps = depth_grad(plan, scale, branch_mask, grad_pre, points, spread)
    output = place_output(plan, all_to_all(output_tiles))
    shares = plane_sum(plan, branch_mask, taps, parts)
    shares = [shares[0]] + [flip_branch(shares[hop], hop) for hop in range(1, branches)]
    share = sum(value.astype(f32) for value in shares)
    if groups is not None:
        peers = [list(range(s, strips, GROUP)) for s in range(GROUP)]
        share = lax.psum(share, "strip", axis_index_groups=peers)
    chunks = lax.all_gather(share.astype(bf16), "strip", axis=0, axis_index_groups=groups)
    joining_total, point_total, depth_total = place_grads(plan, branch_mask, chunks)
    return (jnp.swapaxes(output, 1, 2), joining_total, point_total, depth_total)


def solution(mesh):
    placed = (
        P("strip", None, None),
        P("strip", None, "branch"),
        P("branch", None, None),
        P("branch", None, None),
        P("branch", None),
        P(),
    )
    return jax.shard_map(
        per_device,
        mesh=mesh,
        in_specs=placed,
        out_specs=(
            P("strip", None, "branch"),
            P("branch", None),
            P("branch", None, None),
            P("branch", None, None),
        ),
        check_vma=False,
    )
```

```python
import functools
import math

import jax
import jax.numpy as jnp
from jax import lax
from jax.experimental import pallas as pl
from jax.experimental.pallas import tpu as pltpu
from jax.sharding import PartitionSpec as P

DILATION_STEP = 6
GROUP = 8
CHIPS = 4
JOIN_COST = 1 << 30
DEPTHWISE_COST = 1 << 31
SLOTS = 3

tanh_coef = 0.7978845608
cubic_coef = 0.044715
slope_coef = 0.134145

f32, bf16, i32 = jnp.float32, jnp.bfloat16, jnp.int32
VMEM = pl.BlockSpec(memory_space=pltpu.VMEM)
SMEM = pl.BlockSpec(memory_space=pltpu.SMEM)
ANY = pl.BlockSpec(memory_space=pl.ANY)
HBM = pl.BlockSpec(memory_space=pltpu.HBM)


def gelu_both(values):
    square = values * values
    inner = jnp.tanh(tanh_coef * (values + cubic_coef * values * square))
    half = 0.5 * (1.0 + inner)
    slope = half + 0.5 * values * (1.0 - inner * inner) * tanh_coef * (1.0 + slope_coef * square)
    return values * half, slope


def dot(left, right, dims=((1,), (0,))):
    return lax.dot_general(left, right, (dims, ((), ())), preferred_element_type=f32)


def iota(shape, dim):
    return lax.broadcasted_iota(i32, shape, dim)


def one_hot(mask):
    return jnp.where(mask, 1.0, 0.0).astype(bf16)


class Plan:
    def __init__(self, row_count, col_count, chan_count, width, branches):
        self.rows, self.cols, self.chans, self.width, self.branches = row_count, col_count, chan_count, width, branches
        self.classes = DILATION_STEP
        self.run = col_count // DILATION_STEP
        self.work = col_count // (branches * CHIPS)
        self.taps_t = row_count // 2
        self.sub_rows = GROUP * self.taps_t
        self.pixels = self.sub_rows * self.work
        self.lanes = chan_count // 128
        self.window = max(self.segments(m)[5] for m in range(branches * CHIPS))
        self.piece = self.window * self.taps_t
        self.part = width // branches
        self.step_rows = DILATION_STEP // 2
        self.pad = -(-self.step_rows * branches // 16) * 16
        self.tall = self.pad + self.sub_rows + self.pad
        self.grad_rows = (width + chan_count) // GROUP
        self.join_rows = width // GROUP
        self.point_rows = chan_count // GROUP
        self.tile = 2 * self.work
        self.depth_rows = -(-9 * self.lanes // GROUP // 8) * 8
        self.wide = -(-self.cols // 128) * 128

    def segments(self, m):
        smaller, larger = (min, max) if isinstance(m, int) else (jnp.minimum, jnp.maximum)
        first = m * self.work
        klass = first // self.run
        start = first - klass * self.run
        length = smaller(self.work, self.run - start)
        low = larger(0, start - self.branches)
        size = smaller(self.run, start + length + self.branches) - low
        rest = self.work - length
        if isinstance(m, int):
            total = size + (min(self.run, rest + self.branches) if rest else 0)
        else:
            total = size + jnp.where(rest > 0, jnp.minimum(self.run, rest + self.branches), 0)
        return klass, start, length, low, size, total

    def column(self, m, w):
        klass, start, length, _, _, _ = self.segments(m)
        return jnp.where(w < length, self.classes * (start + w) + klass, self.classes * (w - length) + klass + 1)

    def window_column(self, m, j):
        klass, _, _, low, size, total = self.segments(m)
        inside = jnp.where(j < size, self.classes * (low + j) + klass, self.classes * (j - size) + klass + 1)
        return jnp.where(j < total, inside, -(1 << 20))

    def neighbour(self, segments, w, shift):
        _, start, length, low, size, _ = segments
        first = w < length
        place = jnp.where(first, start + w, w - length) + shift
        found = jnp.where(first, place - low, size + place)
        return jnp.where(jnp.logical_and(place >= 0, place < self.run), found, self.window)


def whereabouts():
    strip = lax.axis_index("strip") % GROUP
    return lax.axis_index("branch"), strip, strip // 2, strip % 2


def slots_of(mask_ref, branches):
    slots, count = [], 0
    for branch in range(branches):
        slots.append(jnp.minimum(count, SLOTS - 1) + 0 * mask_ref[branch])
        count = count + mask_ref[branch]
    return slots, count


def pick(values, index):
    result = values[0]
    for place in range(1, len(values)):
        result = jnp.where(index == place, values[place], result)
    return result


def tile_selector(plan):
    blocks = []
    for chip in range(CHIPS):
        for plane in range(plan.branches):
            row = iota((plan.tile, 128), 0)
            column = plan.column(plane * CHIPS + chip, row // 2)
            blocks.append(column + (row % 2) * plan.wide)
    target = jnp.concatenate(blocks, 0)
    lane = iota(target.shape, 1)
    return jnp.concatenate([one_hot(target == lane + 128 * k) for k in range(2 * plan.wide // 128)], 1)


def halve_kernel(plan, point_ref, joining_ref, half_ref, sems):
    _, _, _, core = whereabouts()
    half_point, half_join = plan.chans // 2, plan.width // 2
    copies = [
        pltpu.make_async_copy(
            point_ref.at[0, pl.ds(pl.multiple_of(core * half_point, half_point), half_point)],
            half_ref.at[pl.ds(0, half_point)],
            sems.at[0],
        ),
        pltpu.make_async_copy(
            joining_ref.at[pl.ds(pl.multiple_of(core * half_join, half_join), half_join)],
            half_ref.at[pl.ds(half_point, half_join)],
            sems.at[1],
        ),
    ]
    for copy in copies:
        copy.start()
    for copy in copies:
        copy.wait()


def halve_weights(plan, point, joining):
    return pl.pallas_call(
        functools.partial(halve_kernel, plan),
        out_shape=jax.ShapeDtypeStruct(((plan.chans + plan.width) // 2, plan.width), bf16),
        in_specs=[HBM] * 2,
        out_specs=VMEM,
        scratch_shapes=[pltpu.SemaphoreType.DMA((2,))],
        compiler_params=pltpu.CompilerParams(vmem_limit_bytes=8 << 20),
        name="halve_weights",
    )(point, joining)


def spread_kernel(plan, features_ref, keep_ref, send_ref):
    plane, _, _, core = whereabouts()
    depth = plan.taps_t * plan.cols
    targets = []
    for chip in range(CHIPS):
        row = iota((plan.piece, 128), 0)
        column = plan.window_column(plane * CHIPS + chip, row // plan.taps_t)
        targets.append(column + (row % plan.taps_t) * plan.cols)
    target = jnp.concatenate(targets, 0)
    lane = iota(target.shape, 1)
    chosen = jnp.concatenate([one_hot(target == lane + 128 * k) for k in range(depth // 128)], 1)
    for flip, out_ref in enumerate((keep_ref, send_ref)):
        rows = jnp.concatenate([features_ref[2 * t + (core ^ flip)] for t in range(plan.taps_t)], 0)
        found = dot(chosen, rows).astype(bf16)
        for chip in range(CHIPS):
            out_ref[chip] = found[chip * plan.piece:(chip + 1) * plan.piece]


def spread_features(plan, features):
    half = jax.ShapeDtypeStruct((CHIPS, plan.piece, plan.chans), bf16)
    return pl.pallas_call(
        functools.partial(spread_kernel, plan),
        out_shape=[half, half],
        in_specs=[VMEM],
        out_specs=[VMEM] * 2,
        compiler_params=pltpu.CompilerParams(vmem_limit_bytes=16 << 20),
        name="spread_features",
    )(features)


def join_kernel(plan, keep_ref, other_ref, *out_refs):
    _, _, chip, _ = whereabouts()
    for hop in range(CHIPS):
        out_refs[hop][0:plan.piece] = keep_ref[chip ^ hop]
        out_refs[hop][plan.piece:] = other_ref[chip ^ hop]


def join_features(plan, keep, other):
    return pl.pallas_call(
        functools.partial(join_kernel, plan),
        out_shape=[jax.ShapeDtypeStruct((2 * plan.piece, plan.chans), bf16)] * CHIPS,
        in_specs=[VMEM] * 2,
        out_specs=[VMEM] * CHIPS,
        compiler_params=pltpu.CompilerParams(vmem_limit_bytes=8 << 20),
        name="join_features",
    )(keep, other)


def send_cotangent_kernel(plan, cotangent_ref, depth_ref, tiles_ref, cotangent, depth, taps, sems):
    _, strip, _, _ = whereabouts()
    copies = [
        pltpu.make_async_copy(cotangent_ref, cotangent, sems.at[0]),
        pltpu.make_async_copy(depth_ref, depth, sems.at[1]),
    ]
    for copy in copies:
        copy.start()
    chosen = tile_selector(plan)
    for copy in copies:
        copy.wait()

    taps[...] = jnp.zeros_like(taps)
    values = depth[0].astype(f32)
    for tap in range(9):
        for group in range(plan.lanes):
            row = tap * plan.lanes + group
            taps[row:row + 1] = values[tap:tap + 1, group * 128:(group + 1) * 128]
    share = taps[pl.ds(pl.multiple_of(strip * plan.depth_rows, 8), plan.depth_rows)]
    fill = jnp.zeros((plan.part, plan.wide - plan.cols), f32)
    blocks = []
    for parity in range(2):
        for high in range(2):
            rows = []
            for low in range(2):
                rows += [cotangent[2 * (2 * high + low) + parity].astype(f32), fill]
            blocks.append(jnp.concatenate(rows, 1))
    found = dot(chosen, jnp.concatenate(blocks, 0).astype(bf16), ((1,), (1,)))
    for chip in range(CHIPS):
        for parity in range(2):
            for plane in range(plan.branches):
                at = (chip * plan.branches + plane) * plan.tile
                tile = found[at:at + plan.tile, parity * 128:(parity + 1) * 128]
                tiles_ref[(2 * chip + parity) * plan.branches + plane] = jnp.concatenate([tile, share], 0).astype(bf16)


def send_cotangent(plan, cotangent, depth):
    return pl.pallas_call(
        functools.partial(send_cotangent_kernel, plan),
        out_shape=jax.ShapeDtypeStruct((GROUP * plan.branches, plan.tile + plan.depth_rows, 128), bf16),
        in_specs=[HBM] * 2,
        out_specs=VMEM,
        scratch_shapes=[
            pltpu.VMEM(cotangent.shape, bf16),
            pltpu.VMEM(depth.shape, bf16),
            pltpu.VMEM((GROUP * plan.depth_rows, 128), f32),
            pltpu.SemaphoreType.DMA((2,)),
        ],
        compiler_params=pltpu.CompilerParams(vmem_limit_bytes=16 << 20),
        cost_estimate=pl.CostEstimate(flops=1, bytes_accessed=1, transcendentals=0),
        name="send_cotangent",
    )(cotangent, depth)


def place_output_kernel(plan, tiles_ref, out_ref, token_ref):
    token_ref[...] = jnp.zeros_like(token_ref)
    chosen = tile_selector(plan)
    halves = []
    for parity in range(2):
        blocks = []
        for chip in range(CHIPS):
            for plane in range(plan.branches):
                blocks.append(tiles_ref[(2 * chip + parity) * plan.branches + plane].astype(f32))
        halves.append(jnp.concatenate(blocks, 0))
    found = dot(jnp.concatenate(halves, 1).astype(bf16), chosen, ((0,), (0,))).astype(bf16)
    for parity in range(2):
        for high in range(2):
            for low in range(2):
                at = parity * 128 + high * plan.part
                out_ref[2 * (2 * high + low) + parity] = found[
                    at:at + plan.part, low * plan.wide:low * plan.wide + plan.cols
                ]


def place_output(plan, tiles):
    return pl.pallas_call(
        functools.partial(place_output_kernel, plan),
        out_shape=[
            jax.ShapeDtypeStruct((plan.rows, plan.part, plan.cols), bf16),
            jax.ShapeDtypeStruct((8, 128), f32),
        ],
        in_specs=[VMEM],
        out_specs=[VMEM] * 2,
        compiler_params=pltpu.CompilerParams(vmem_limit_bytes=16 << 20),
        name="place_output",
    )(tiles)


def swap_halves(left, right):
    low = iota(left.shape, 1) < 64
    return (
        jnp.where(low, left, pltpu.roll(right, 64, 1)),
        jnp.where(low, pltpu.roll(left, 64, 1), right),
    )


class Copies:
    def __init__(self, sems):
        self.sems, self.all = sems, []

    def start(self, source, target):
        copy = pltpu.make_async_copy(source, target, self.sems.at[len(self.all)])
        copy.start()
        self.all.append(copy)

    def wait(self):
        for copy in self.all:
            copy.wait()
        self.all = []


def depthwise_kernel(plan, halo, mask_ref, tiles_ref, *refs):
    piece_refs, refs = refs[:CHIPS], refs[CHIPS:]
    halo_refs, refs = (refs[:2], refs[2:]) if halo else ((), refs)
    dw_out, spread, cotangent_ref, order_ref, token, pieces, halo_pieces, sorted_rows, sems = refs
    token[...] = jnp.zeros_like(token)
    plane, _, chip, core = whereabouts()
    copies = Copies(sems)
    for hop in range(CHIPS):
        for flip in range(2):
            copies.start(
                piece_refs[hop].at[pl.ds(flip * plan.piece, plan.piece)], pieces.at[2 * (chip ^ hop) + (core ^ flip)]
            )
    for place, ref in enumerate(halo_refs):
        copies.start(ref, halo_pieces.at[place])

    for group in range(plan.lanes):
        edge = jnp.zeros((plan.window, plan.pad, 128), f32)
        spread[group, 0:plan.window, 0:plan.pad] = edge
        spread[group, 0:plan.window, plan.pad + plan.sub_rows:plan.tall] = edge
        spread[group, plan.window] = jnp.zeros((plan.tall, 128), f32)

    low_rows = iota((8, 128), 0) < 4

    def lay(source, place, row):
        @pl.loop(0, plan.piece // 16)
        def _(quad):
            at = pl.multiple_of(quad * 16, 16)
            for group in range(plan.lanes):
                lanes = pl.ds(group * 128, 128)
                upper = source[place, pl.ds(at, 16), lanes].astype(f32)
                lower = source[place + 1, pl.ds(at, 16), lanes].astype(f32)
                for part in range(2):
                    a, b = upper[8 * part:8 * part + 8], lower[8 * part:8 * part + 8]
                    column = quad * 4 + 2 * part
                    spread[group, column, row:row + 8] = jnp.where(low_rows, a, pltpu.roll(b, 4, 0))
                    spread[group, column + 1, row:row + 8] = jnp.where(low_rows, pltpu.roll(a, 4, 0), b)

    copies.wait()
    for pair in range(CHIPS):
        lay(pieces, 2 * pair, plan.pad + 8 * pair)
    if halo:
        for pair in range(2):
            lay(halo_pieces.at[0], 2 * pair, plan.pad - 16 + 8 * pair)
            lay(halo_pieces.at[1], 2 * pair, plan.pad + plan.sub_rows + 8 * pair)

    segments = plan.segments(plane * CHIPS + chip)
    for branch in range(plan.branches):
        @pl.when(mask_ref[branch] > 0)
        def _():
            shares = [
                tiles_ref[strip * plan.branches + branch].astype(f32)
                for strip in range(-(-9 * plan.lanes // plan.depth_rows))
            ]
            for group in range(plan.lanes):
                kernel = []
                for tap in range(9):
                    row = tap * plan.lanes + group
                    at = plan.tile + row % plan.depth_rows
                    kernel.append(jnp.broadcast_to(shares[row // plan.depth_rows][at:at + 1], (plan.sub_rows, 128)))

                @pl.loop(0, plan.work)
                def _(w):
                    total = None
                    for j in range(3):
                        column = plan.neighbour(segments, w, (j - 1) * (branch + 1))
                        for i in range(3):
                            row = plan.pad + (i - 1) * plan.step_rows * (branch + 1)
                            term = spread[group, column, row:row + plan.sub_rows] * kernel[3 * i + j]
                            total = term if total is None else total + term
                    at = pl.multiple_of(w * plan.sub_rows, plan.sub_rows)
                    dw_out[branch, pl.ds(at, plan.sub_rows), group * 128:(group + 1) * 128] = total.astype(bf16)

    pixel = iota((plan.pixels, 128), 0)
    column = pixel // plan.sub_rows
    row = pixel - column * plan.sub_rows
    source = (row // 2) * plan.tile + 2 * column + row % 2
    lane = iota(source.shape, 1)
    order = jnp.concatenate([one_hot(source == lane + 128 * k) for k in range(plan.pixels // 128)], 1)
    for pair in range(GROUP):
        for couple in range(plan.branches // 2):
            left = tiles_ref[pair * plan.branches + 2 * couple].astype(f32)[:plan.tile]
            right = tiles_ref[pair * plan.branches + 2 * couple + 1].astype(f32)[:plan.tile]
            first, second = swap_halves(left, right)
            lanes = pl.ds(couple * 128, 128)
            sorted_rows[pl.ds(2 * pair * plan.tile, plan.tile), lanes] = first
            sorted_rows[pl.ds((2 * pair + 1) * plan.tile, plan.tile), lanes] = second
    cotangent_ref[...] = dot(order, sorted_rows[...].astype(bf16))
    order_ref[...] = order


def depthwise(plan, mask, tiles, pieces, halos):
    operands = [mask, tiles, *pieces, *halos]
    return pl.pallas_call(
        functools.partial(depthwise_kernel, plan, len(halos) > 0),
        out_shape=[
            jax.ShapeDtypeStruct((plan.branches, plan.pixels, plan.chans), bf16),
            jax.ShapeDtypeStruct((plan.lanes, plan.window + 1, plan.tall, 128), f32),
            jax.ShapeDtypeStruct((plan.pixels, plan.width), f32),
            jax.ShapeDtypeStruct((plan.pixels, plan.pixels), bf16),
            jax.ShapeDtypeStruct((8, 128), f32),
        ],
        in_specs=[SMEM, VMEM] + [ANY] * (len(operands) - 2),
        out_specs=[VMEM] * 5,
        scratch_shapes=[
            pltpu.VMEM((GROUP, plan.piece, plan.chans), bf16),
            pltpu.VMEM((2, 4, plan.piece, plan.chans) if halos else (16, 128), bf16),
            pltpu.VMEM((plan.pixels, plan.width), f32),
            pltpu.SemaphoreType.DMA((GROUP + 2,)),
        ],
        compiler_params=pltpu.CompilerParams(vmem_limit_bytes=20 << 20),
        cost_estimate=pl.CostEstimate(flops=DEPTHWISE_COST, bytes_accessed=1 << 10, transcendentals=0),
        name="depthwise",
    )(*operands)


def join_weights_kernel(plan, point_ref, joining_ref, *refs):
    mine_refs, other_refs = refs[:plan.branches - 1], refs[plan.branches - 1:2 * plan.branches - 2]
    point, joining, sems = refs[-3:]
    plane, _, _, core = whereabouts()
    copies = Copies(sems)
    copies.start(point_ref.at[0], point.at[plane])
    copies.start(joining_ref, joining.at[plane])
    half_point, half_join = plan.chans // 2, plan.width // 2
    for hop in range(1, plan.branches):
        for side, ref in ((core, mine_refs[hop - 1]), (1 - core, other_refs[hop - 1])):
            at_point = pl.multiple_of(side * half_point, half_point)
            at_join = pl.multiple_of(side * half_join, half_join)
            copies.start(ref.at[pl.ds(0, half_point)], point.at[plane ^ hop, pl.ds(at_point, half_point)])
            copies.start(ref.at[pl.ds(half_point, half_join)], joining.at[plane ^ hop, pl.ds(at_join, half_join)])
    copies.wait()


def join_weights(plan, point, joining, mine, others, token):
    return pl.pallas_call(
        functools.partial(join_weights_kernel, plan),
        out_shape=[
            jax.ShapeDtypeStruct((plan.branches, plan.chans, plan.width), bf16),
            jax.ShapeDtypeStruct((plan.branches, plan.width, plan.width), bf16),
        ],
        in_specs=[ANY] * (3 + len(mine) + len(others)),
        out_specs=[VMEM] * 2,
        scratch_shapes=[pltpu.SemaphoreType.DMA((4 * plan.branches,))],
        compiler_params=pltpu.CompilerParams(vmem_limit_bytes=8 << 20),
        cost_estimate=pl.CostEstimate(flops=JOIN_COST, bytes_accessed=1 << 20, transcendentals=0),
        name="join_weights",
    )(point, joining, *mine, *others, token)


def main_kernel(plan, scale, mask_ref, dw_out, cotangent_ref, order_ref, point, joining,
                output_ref, keep_ref, send_ref, grad_pre_ref, branch_out, slope, joined, sorted_rows):
    branches, width, chans = plan.branches, plan.width, plan.chans
    _, _, _, core = whereabouts()
    slots, active_count = slots_of(mask_ref, branches)
    joined[...] = jnp.zeros_like(joined)

    @pl.loop(0, branches)
    def _(branch):
        @pl.when(mask_ref[branch] > 0)
        def _():
            value, derivative = gelu_both(dot(dw_out[branch], point[branch]))
            value = value.astype(bf16)
            branch_out[branch] = value
            slope[branch] = derivative
            joined[...] += dot(value, joining[branch])

    value, derivative = gelu_both(joined[...])
    grad_joined = (cotangent_ref[...] * derivative).astype(bf16)

    def store_grads(slot, part, first, rows):
        at = pl.multiple_of(slot * plan.grad_rows + first, 32)
        for half in range(2):
            for kept, ref in ((True, keep_ref), (False, send_ref)):
                @pl.when((core == half) == kept)
                def _():
                    for chip in range(CHIPS):
                        chunk = half * CHIPS + chip
                        ref[chip, pl.ds(at, rows)] = part[chunk * rows:(chunk + 1) * rows]

    @pl.loop(0, branches)
    def _(branch):
        @pl.when(mask_ref[branch] > 0)
        def _():
            slot = pick(slots, branch)
            joining_part = (dot(branch_out[branch], grad_joined, ((0,), (0,))) * scale).astype(bf16)
            store_grads(slot, joining_part, 0, plan.join_rows)
            grad_branch = dot(grad_joined, joining[branch], ((1,), (1,)))
            grad_pre = (grad_branch * slope[branch]).astype(bf16)
            grad_pre_ref[branch] = grad_pre
            point_part = (dot(dw_out[branch], grad_pre, ((0,), (0,))) * scale).astype(bf16)
            store_grads(slot, point_part, plan.join_rows, plan.point_rows)

    for slot in range(1, SLOTS):
        @pl.when(slot >= active_count)
        def _():
            rows = pl.ds(slot * plan.grad_rows, plan.grad_rows)
            empty = jnp.zeros((plan.grad_rows, width), bf16)
            for chip in range(CHIPS):
                keep_ref[chip, rows] = empty
                send_ref[chip, rows] = empty

    sorted_rows[...] = dot(order_ref[...], value.astype(bf16), ((0,), (0,)))
    for pair in range(GROUP):
        for couple in range(branches // 2):
            lanes = pl.ds(couple * 128, 128)
            left = sorted_rows[pl.ds(2 * pair * plan.tile, plan.tile), lanes]
            right = sorted_rows[pl.ds((2 * pair + 1) * plan.tile, plan.tile), lanes]
            first, second = swap_halves(left, right)
            output_ref[pair * branches + 2 * couple] = first.astype(bf16)
            output_ref[pair * branches + 2 * couple + 1] = second.astype(bf16)


def main_step(plan, scale, mask, dw_out, cotangent, order, point, joining):
    half = jax.ShapeDtypeStruct((GROUP // 2, SLOTS * plan.grad_rows, plan.width), bf16)
    return pl.pallas_call(
        functools.partial(main_kernel, plan, scale),
        out_shape=[
            jax.ShapeDtypeStruct((GROUP * plan.branches, plan.tile, 128), bf16),
            half,
            half,
            jax.ShapeDtypeStruct((plan.branches, plan.pixels, plan.width), bf16),
        ],
        in_specs=[SMEM] + [VMEM] * 5,
        out_specs=[VMEM] * 4,
        scratch_shapes=[
            pltpu.VMEM((plan.branches, plan.pixels, plan.width), bf16),
            pltpu.VMEM((plan.branches, plan.pixels, plan.width), f32),
            pltpu.VMEM((plan.pixels, plan.width), f32),
            pltpu.VMEM((plan.pixels, plan.width), f32),
        ],
        compiler_params=pltpu.CompilerParams(vmem_limit_bytes=24 << 20),
        cost_estimate=pl.CostEstimate(flops=1 << 31, bytes_accessed=1 << 24, transcendentals=0),
        name="forward_and_backward",
    )(mask, dw_out, cotangent, order, point, joining)


def depth_grad_kernel(plan, scale, mask_ref, grad_pre_ref, point, spread, out_ref, grad_dw, rows):
    plane, _, chip, _ = whereabouts()
    slots, _ = slots_of(mask_ref, plan.branches)
    segments = plan.segments(plane * CHIPS + chip)
    out_ref[...] = jnp.zeros_like(out_ref)
    rows[...] = jnp.zeros_like(rows)
    for branch in range(plan.branches):
        @pl.when(mask_ref[branch] > 0)
        def _():
            grad_pre = grad_pre_ref[branch]
            for group in range(plan.lanes):
                grad_dw[group] = dot(grad_pre, point[branch, group * 128:(group + 1) * 128], ((1,), (1,)))
            for group in range(plan.lanes):
                def add_column(w, sums):
                    at = pl.multiple_of(w * plan.sub_rows, plan.sub_rows)
                    given = grad_dw[group, pl.ds(at, plan.sub_rows)]
                    sums = list(sums)
                    for j in range(3):
                        column = plan.neighbour(segments, w, (j - 1) * (branch + 1))
                        for i in range(3):
                            row = plan.pad + (i - 1) * plan.step_rows * (branch + 1)
                            product = spread[group, column, row:row + plan.sub_rows] * given
                            for part in range(plan.sub_rows // 8):
                                sums[3 * i + j] = sums[3 * i + j] + product[8 * part:8 * part + 8]
                    return tuple(sums)

                sums = lax.fori_loop(0, plan.work, add_column, (jnp.zeros((8, 128), f32),) * 9)
                lanes = slice((group % 2) * 128, (group % 2) * 128 + 128)
                for tap in range(9):
                    row = 2 * tap + group // 2
                    rows[row:row + 1, lanes] = jnp.sum(sums[tap], axis=0, keepdims=True) * scale
            out_ref[slots[branch]] = rows[...].astype(bf16)


def depth_grad(plan, scale, mask, grad_pre, point, spread):
    return pl.pallas_call(
        functools.partial(depth_grad_kernel, plan, scale),
        out_shape=jax.ShapeDtypeStruct((SLOTS, 32, plan.width), bf16),
        in_specs=[SMEM] + [VMEM] * 3,
        out_specs=VMEM,
        scratch_shapes=[
            pltpu.VMEM((plan.lanes, plan.pixels, 128), f32),
            pltpu.VMEM((32, plan.width), f32),
        ],
        compiler_params=pltpu.CompilerParams(vmem_limit_bytes=24 << 20),
        cost_estimate=pl.CostEstimate(flops=1 << 26, bytes_accessed=1 << 24, transcendentals=0),
        name="depth_grad",
    )(mask, grad_pre, point, spread)


def chip_sum_kernel(keep_ref, other_ref, *out_refs):
    _, _, chip, _ = whereabouts()
    for hop in range(CHIPS):
        out_refs[hop][...] = (keep_ref[chip ^ hop].astype(f32) + other_ref[chip ^ hop].astype(f32)).astype(bf16)


def chip_sum(keep, other):
    return pl.pallas_call(
        chip_sum_kernel,
        out_shape=[jax.ShapeDtypeStruct(keep.shape[1:], bf16)] * CHIPS,
        in_specs=[VMEM] * 2,
        out_specs=[VMEM] * CHIPS,
        compiler_params=pltpu.CompilerParams(vmem_limit_bytes=16 << 20),
        name="chip_sum",
    )(keep, other)


def plane_sum_kernel(plan, mask_ref, depth_ref, *refs):
    total, out_refs = refs[-1], refs[CHIPS:-1]
    plane, _, _, _ = whereabouts()
    slots, _ = slots_of(mask_ref, plan.branches)
    added = refs[0][...].astype(f32)
    for ref in refs[1:CHIPS]:
        added = added + ref[...].astype(f32)
    total[...] = added
    rows = plan.grad_rows
    for hop in range(plan.branches):
        slot = pick(slots, plane ^ hop)
        out_refs[hop][0:rows] = total[pl.ds(pl.multiple_of(slot * rows, 32), rows)].astype(bf16)
        out_refs[hop][rows:] = depth_ref[slot]


def plane_sum(plan, mask, depth, parts):
    return pl.pallas_call(
        functools.partial(plane_sum_kernel, plan),
        out_shape=[jax.ShapeDtypeStruct((plan.grad_rows + depth.shape[1], plan.width), bf16)] * plan.branches,
        in_specs=[SMEM] + [VMEM] * (1 + CHIPS),
        out_specs=[VMEM] * plan.branches,
        scratch_shapes=[pltpu.VMEM(parts[0].shape, f32)],
        compiler_params=pltpu.CompilerParams(vmem_limit_bytes=16 << 20),
        name="plane_sum",
    )(mask, depth, *parts)


def place_grads_kernel(plan, mask_ref, *refs):
    chunk_refs, (joining_ref, point_ref, depth_ref) = refs[:GROUP], refs[GROUP + 1:]
    plane, _, chip, core = whereabouts()
    active = pick([mask_ref[branch] for branch in range(plan.branches)], plane) > 0
    rows = plan.grad_rows
    taps = None
    for flip in range(2):
        for hop in range(CHIPS):
            chunk = jnp.where(active, chunk_refs[flip * CHIPS + hop][...].astype(f32), 0.0)
            at = (core ^ flip) * CHIPS + (chip ^ hop)
            joining_ref[pl.ds(pl.multiple_of(at * plan.join_rows, plan.join_rows), plan.join_rows)] = chunk[:plan.join_rows]
            place = pl.multiple_of(at * plan.point_rows, plan.point_rows)
            point_ref[0, pl.ds(place, plan.point_rows)] = chunk[plan.join_rows:rows]
            taps = chunk[rows:] if taps is None else taps + chunk[rows:]
    for tap in range(9):
        for group in range(plan.lanes):
            row, lane = 2 * tap + group // 2, (group % 2) * 128
            depth_ref[0, tap:tap + 1, group * 128:(group + 1) * 128] = taps[row:row + 1, lane:lane + 128]


def place_grads(plan, mask, chunks, token):
    return pl.pallas_call(
        functools.partial(place_grads_kernel, plan),
        out_shape=[
            jax.ShapeDtypeStruct((plan.width, plan.width), f32),
            jax.ShapeDtypeStruct((1, plan.chans, plan.width), f32),
            jax.ShapeDtypeStruct((1, 9, plan.chans), f32),
        ],
        in_specs=[SMEM] + [VMEM] * GROUP + [ANY],
        out_specs=[VMEM] * 3,
        compiler_params=pltpu.CompilerParams(vmem_limit_bytes=16 << 20),
        name="place_grads",
    )(mask, *chunks, token)


def per_device(features, cotangent, depth_weight, point_weight, joining_weight, branch_mask):
    row_count, col_count, chan_count = features.shape
    strips = lax.axis_size("strip")
    branches = lax.axis_size("branch")
    width = joining_weight.shape[1]
    plan = Plan(row_count, col_count, chan_count, width, branches)
    scale = 1.0 / math.sqrt(row_count * col_count * strips)
    groups = None if strips == GROUP else [list(range(g, g + GROUP)) for g in range(0, strips, GROUP)]

    def flip_strip(value, hop):
        return lax.ppermute(value, "strip", [(s, s ^ hop) for s in range(strips)])

    def flip_branch(value, hop):
        return lax.ppermute(value, "branch", [(b, b ^ hop) for b in range(branches)])

    def all_to_all(tiles):
        if groups is None:
            return lax.all_to_all(tiles, ("strip", "branch"), 0, 0, tiled=True)
        tiles = tiles.reshape(GROUP, branches, *tiles.shape[1:])
        tiles = lax.all_to_all(tiles, "branch", 1, 1, tiled=True)
        tiles = lax.all_to_all(tiles, "strip", 0, 0, tiled=True, axis_index_groups=groups)
        return tiles.reshape(GROUP * branches, *tiles.shape[2:])

    half = halve_weights(plan, point_weight, joining_weight)
    mine = [flip_branch(half, 1), flip_branch(half, 2)]
    mine.append(flip_branch(mine[1], 1))

    keep, send = spread_features(plan, features)
    joint = join_features(plan, keep, flip_strip(send, 1))
    pieces = [joint[0]] + [flip_strip(joint[hop], 2 * hop) for hop in range(1, CHIPS)]
    halos = []
    if groups is not None:
        strip = lax.axis_index("strip") % GROUP
        near = jnp.stack(pieces).reshape(CHIPS, 2, plan.piece, plan.chans)
        at = jnp.arange(GROUP)
        near = near[(at // 2) ^ (strip // 2), (at % 2) ^ (strip % 2)]
        down = [(s, s + GROUP) for s in range(strips - GROUP)]
        up = [(s + GROUP, s) for s in range(strips - GROUP)]
        halos = [lax.ppermute(near[GROUP - 4:], "strip", down), lax.ppermute(near[:4], "strip", up)]
    tiles = all_to_all(send_cotangent(plan, jnp.swapaxes(cotangent, 1, 2), depth_weight))
    dw_out, spread, pixel_cotangent, order, token = depthwise(plan, branch_mask, tiles, pieces, halos)

    mine, token = lax.optimization_barrier((mine, token))
    others = [flip_strip(value, 1) for value in mine]
    points, joinings = join_weights(plan, point_weight, joining_weight, mine, others, token)
    output_tiles, keep, send, grad_pre = main_step(
        plan, scale, branch_mask, dw_out, pixel_cotangent, order, points, joinings
    )
    parts = chip_sum(keep, flip_strip(send, 1))
    parts, output_tiles, grad_pre = lax.optimization_barrier((parts, output_tiles, grad_pre))
    parts = [parts[0]] + [flip_strip(parts[hop], 2 * hop) for hop in range(1, CHIPS)]
    taps = depth_grad(plan, scale, branch_mask, grad_pre, points, spread)
    output, token = place_output(plan, all_to_all(output_tiles))
    shares = plane_sum(plan, branch_mask, taps, parts)
    shares = [shares[0]] + [flip_branch(shares[hop], hop) for hop in range(1, branches)]
    share = sum(value.astype(f32) for value in shares)
    if groups is not None:
        peers = [list(range(s, strips, GROUP)) for s in range(GROUP)]
        share = lax.psum(share, "strip", axis_index_groups=peers)
    share = share.astype(bf16)
    chunks = [share] + [flip_strip(share, 2 * hop) for hop in range(1, CHIPS)]
    chunks = chunks + [flip_strip(chunk, 1) for chunk in chunks]
    joining_total, point_total, depth_total = place_grads(plan, branch_mask, chunks, token)
    return (jnp.swapaxes(output, 1, 2), joining_total, point_total, depth_total)


def solution(mesh):
    placed = (
        P("strip", None, None),
        P("strip", None, "branch"),
        P("branch", None, None),
        P("branch", None, None),
        P("branch", None),
        P(),
    )
    return jax.shard_map(
        per_device,
        mesh=mesh,
        in_specs=placed,
        out_specs=(
            P("strip", None, "branch"),
            P("branch", None),
            P("branch", None, None),
            P("branch", None, None),
        ),
        check_vma=False,
    )
```

```python
import functools
import math

import jax
import jax.numpy as jnp
from jax import lax
from jax.experimental import pallas as pl
from jax.experimental.pallas import tpu as pltpu
from jax.sharding import PartitionSpec as P

DILATION_STEP = 6
GROUP = 8
CHIPS = 4
DEPTHWISE_COST = 1 << 31
SLOTS = 3

tanh_coef = 0.7978845608
cubic_coef = 0.044715
slope_coef = 0.134145

f32, bf16, i32 = jnp.float32, jnp.bfloat16, jnp.int32
VMEM = pl.BlockSpec(memory_space=pltpu.VMEM)
SMEM = pl.BlockSpec(memory_space=pltpu.SMEM)
ANY = pl.BlockSpec(memory_space=pl.ANY)
HBM = pl.BlockSpec(memory_space=pltpu.HBM)


def gelu_both(values):
    square = values * values
    inner = jnp.tanh(tanh_coef * (values + cubic_coef * values * square))
    half = 0.5 * (1.0 + inner)
    slope = half + 0.5 * values * (1.0 - inner * inner) * tanh_coef * (1.0 + slope_coef * square)
    return values * half, slope


def dot(left, right, dims=((1,), (0,))):
    return lax.dot_general(left, right, (dims, ((), ())), preferred_element_type=f32)


def iota(shape, dim):
    return lax.broadcasted_iota(i32, shape, dim)


def one_hot(mask):
    return jnp.where(mask, 1.0, 0.0).astype(bf16)


class Plan:
    def __init__(self, row_count, col_count, chan_count, width, branches):
        self.rows, self.cols, self.chans, self.width, self.branches = row_count, col_count, chan_count, width, branches
        self.classes = DILATION_STEP
        self.run = col_count // DILATION_STEP
        self.work = col_count // (branches * CHIPS)
        self.taps_t = row_count // 2
        self.sub_rows = GROUP * self.taps_t
        self.pixels = self.sub_rows * self.work
        self.lanes = chan_count // 128
        self.window = max(self.segments(m)[5] for m in range(branches * CHIPS))
        self.piece = self.window * self.taps_t
        self.part = width // branches
        self.step_rows = DILATION_STEP // 2
        self.pad = -(-self.step_rows * branches // 16) * 16
        self.tall = self.pad + self.sub_rows + self.pad
        self.grad_rows = (width + chan_count) // GROUP
        self.join_rows = width // GROUP
        self.point_rows = chan_count // GROUP
        self.tile = 2 * self.work
        self.depth_rows = -(-9 * self.lanes // GROUP // 8) * 8
        self.wide = -(-self.cols // 128) * 128

    def segments(self, m):
        smaller, larger = (min, max) if isinstance(m, int) else (jnp.minimum, jnp.maximum)
        first = m * self.work
        klass = first // self.run
        start = first - klass * self.run
        length = smaller(self.work, self.run - start)
        low = larger(0, start - self.branches)
        size = smaller(self.run, start + length + self.branches) - low
        rest = self.work - length
        if isinstance(m, int):
            total = size + (min(self.run, rest + self.branches) if rest else 0)
        else:
            total = size + jnp.where(rest > 0, jnp.minimum(self.run, rest + self.branches), 0)
        return klass, start, length, low, size, total

    def column(self, m, w):
        klass, start, length, _, _, _ = self.segments(m)
        return jnp.where(w < length, self.classes * (start + w) + klass, self.classes * (w - length) + klass + 1)

    def window_column(self, m, j):
        klass, _, _, low, size, total = self.segments(m)
        inside = jnp.where(j < size, self.classes * (low + j) + klass, self.classes * (j - size) + klass + 1)
        return jnp.where(j < total, inside, -(1 << 20))

    def neighbour(self, segments, w, shift):
        _, start, length, low, size, _ = segments
        first = w < length
        place = jnp.where(first, start + w, w - length) + shift
        found = jnp.where(first, place - low, size + place)
        return jnp.where(jnp.logical_and(place >= 0, place < self.run), found, self.window)


def whereabouts():
    strip = lax.axis_index("strip") % GROUP
    return lax.axis_index("branch"), strip, strip // 2, strip % 2


def slots_of(mask_ref, branches):
    slots, count = [], 0
    for branch in range(branches):
        slots.append(jnp.minimum(count, SLOTS - 1) + 0 * mask_ref[branch])
        count = count + mask_ref[branch]
    return slots, count


def pick(values, index):
    result = values[0]
    for place in range(1, len(values)):
        result = jnp.where(index == place, values[place], result)
    return result


def tile_selector(plan):
    blocks = []
    for chip in range(CHIPS):
        for plane in range(plan.branches):
            row = iota((plan.tile, 128), 0)
            column = plan.column(plane * CHIPS + chip, row // 2)
            blocks.append(column + (row % 2) * plan.wide)
    target = jnp.concatenate(blocks, 0)
    lane = iota(target.shape, 1)
    return jnp.concatenate([one_hot(target == lane + 128 * k) for k in range(2 * plan.wide // 128)], 1)


def halve_kernel(plan, point_ref, joining_ref, half_ref, sems):
    _, _, _, core = whereabouts()
    half_point, half_join = plan.chans // 2, plan.width // 2
    copies = [
        pltpu.make_async_copy(
            point_ref.at[0, pl.ds(pl.multiple_of(core * half_point, half_point), half_point)],
            half_ref.at[pl.ds(0, half_point)],
            sems.at[0],
        ),
        pltpu.make_async_copy(
            joining_ref.at[pl.ds(pl.multiple_of(core * half_join, half_join), half_join)],
            half_ref.at[pl.ds(half_point, half_join)],
            sems.at[1],
        ),
    ]
    for copy in copies:
        copy.start()
    for copy in copies:
        copy.wait()


def halve_weights(plan, point, joining):
    return pl.pallas_call(
        functools.partial(halve_kernel, plan),
        out_shape=jax.ShapeDtypeStruct(((plan.chans + plan.width) // 2, plan.width), bf16),
        in_specs=[HBM] * 2,
        out_specs=VMEM,
        scratch_shapes=[pltpu.SemaphoreType.DMA((2,))],
        compiler_params=pltpu.CompilerParams(vmem_limit_bytes=8 << 20),
        name="halve_weights",
    )(point, joining)


def spread_kernel(plan, features_ref, keep_ref, send_ref):
    plane, _, _, core = whereabouts()
    depth = plan.taps_t * plan.cols
    targets = []
    for chip in range(CHIPS):
        row = iota((plan.piece, 128), 0)
        column = plan.window_column(plane * CHIPS + chip, row // plan.taps_t)
        targets.append(column + (row % plan.taps_t) * plan.cols)
    target = jnp.concatenate(targets, 0)
    lane = iota(target.shape, 1)
    chosen = jnp.concatenate([one_hot(target == lane + 128 * k) for k in range(depth // 128)], 1)
    for flip, out_ref in enumerate((keep_ref, send_ref)):
        rows = jnp.concatenate([features_ref[2 * t + (core ^ flip)] for t in range(plan.taps_t)], 0)
        found = dot(chosen, rows).astype(bf16)
        for chip in range(CHIPS):
            out_ref[chip] = found[chip * plan.piece:(chip + 1) * plan.piece]


def spread_features(plan, features):
    half = jax.ShapeDtypeStruct((CHIPS, plan.piece, plan.chans), bf16)
    return pl.pallas_call(
        functools.partial(spread_kernel, plan),
        out_shape=[half, half],
        in_specs=[VMEM],
        out_specs=[VMEM] * 2,
        compiler_params=pltpu.CompilerParams(vmem_limit_bytes=16 << 20),
        name="spread_features",
    )(features)


def join_kernel(plan, keep_ref, other_ref, *out_refs):
    _, _, chip, _ = whereabouts()
    for hop in range(CHIPS):
        out_refs[hop][0:plan.piece] = keep_ref[chip ^ hop]
        out_refs[hop][plan.piece:] = other_ref[chip ^ hop]


def join_features(plan, keep, other):
    return pl.pallas_call(
        functools.partial(join_kernel, plan),
        out_shape=[jax.ShapeDtypeStruct((2 * plan.piece, plan.chans), bf16)] * CHIPS,
        in_specs=[VMEM] * 2,
        out_specs=[VMEM] * CHIPS,
        compiler_params=pltpu.CompilerParams(vmem_limit_bytes=8 << 20),
        name="join_features",
    )(keep, other)


def send_cotangent_kernel(plan, cotangent_ref, depth_ref, tiles_ref, cotangent, depth, taps, sems):
    _, strip, _, _ = whereabouts()
    copies = [
        pltpu.make_async_copy(cotangent_ref, cotangent, sems.at[0]),
        pltpu.make_async_copy(depth_ref, depth, sems.at[1]),
    ]
    for copy in copies:
        copy.start()
    chosen = tile_selector(plan)
    for copy in copies:
        copy.wait()

    taps[...] = jnp.zeros_like(taps)
    values = depth[0].astype(f32)
    for tap in range(9):
        for group in range(plan.lanes):
            row = tap * plan.lanes + group
            taps[row:row + 1] = values[tap:tap + 1, group * 128:(group + 1) * 128]
    share = taps[pl.ds(pl.multiple_of(strip * plan.depth_rows, 8), plan.depth_rows)]
    fill = jnp.zeros((plan.part, plan.wide - plan.cols), f32)
    blocks = []
    for parity in range(2):
        for high in range(2):
            rows = []
            for low in range(2):
                rows += [cotangent[2 * (2 * high + low) + parity].astype(f32), fill]
            blocks.append(jnp.concatenate(rows, 1))
    found = dot(chosen, jnp.concatenate(blocks, 0).astype(bf16), ((1,), (1,)))
    for chip in range(CHIPS):
        for parity in range(2):
            for plane in range(plan.branches):
                at = (chip * plan.branches + plane) * plan.tile
                tile = found[at:at + plan.tile, parity * 128:(parity + 1) * 128]
                tiles_ref[(2 * chip + parity) * plan.branches + plane] = jnp.concatenate([tile, share], 0).astype(bf16)


def send_cotangent(plan, cotangent, depth):
    return pl.pallas_call(
        functools.partial(send_cotangent_kernel, plan),
        out_shape=jax.ShapeDtypeStruct((GROUP * plan.branches, plan.tile + plan.depth_rows, 128), bf16),
        in_specs=[HBM] * 2,
        out_specs=VMEM,
        scratch_shapes=[
            pltpu.VMEM(cotangent.shape, bf16),
            pltpu.VMEM(depth.shape, bf16),
            pltpu.VMEM((GROUP * plan.depth_rows, 128), f32),
            pltpu.SemaphoreType.DMA((2,)),
        ],
        compiler_params=pltpu.CompilerParams(vmem_limit_bytes=60 << 20),
        cost_estimate=pl.CostEstimate(flops=1, bytes_accessed=1, transcendentals=0),
        name="send_cotangent",
    )(cotangent, depth)


def place_output_kernel(plan, tiles_ref, out_ref, token_ref):
    token_ref[...] = jnp.zeros_like(token_ref)
    chosen = tile_selector(plan)
    halves = []
    for parity in range(2):
        blocks = []
        for chip in range(CHIPS):
            for plane in range(plan.branches):
                blocks.append(tiles_ref[(2 * chip + parity) * plan.branches + plane].astype(f32))
        halves.append(jnp.concatenate(blocks, 0))
    found = dot(jnp.concatenate(halves, 1).astype(bf16), chosen, ((0,), (0,))).astype(bf16)
    for parity in range(2):
        for high in range(2):
            for low in range(2):
                at = parity * 128 + high * plan.part
                out_ref[2 * (2 * high + low) + parity] = found[
                    at:at + plan.part, low * plan.wide:low * plan.wide + plan.cols
                ]


def place_output(plan, tiles):
    return pl.pallas_call(
        functools.partial(place_output_kernel, plan),
        out_shape=[
            jax.ShapeDtypeStruct((plan.rows, plan.part, plan.cols), bf16),
            jax.ShapeDtypeStruct((8, 128), f32),
        ],
        in_specs=[VMEM],
        out_specs=[VMEM] * 2,
        compiler_params=pltpu.CompilerParams(vmem_limit_bytes=16 << 20),
        name="place_output",
    )(tiles)


def swap_halves(left, right):
    low = iota(left.shape, 1) < 64
    return (
        jnp.where(low, left, pltpu.roll(right, 64, 1)),
        jnp.where(low, pltpu.roll(left, 64, 1), right),
    )


class Copies:
    def __init__(self, sems):
        self.sems, self.all = sems, []

    def start(self, source, target):
        copy = pltpu.make_async_copy(source, target, self.sems.at[len(self.all)])
        copy.start()
        self.all.append(copy)

    def wait(self):
        for copy in self.all:
            copy.wait()
        self.all = []


def depthwise_kernel(plan, halo, mask_ref, tiles_ref, *refs):
    piece_refs, refs = refs[:CHIPS], refs[CHIPS:]
    halo_refs, refs = (refs[:2], refs[2:]) if halo else ((), refs)
    dw_out, spread, cotangent_ref, order_ref, token, pieces, halo_pieces, sorted_rows, sems = refs
    token[...] = jnp.zeros_like(token)
    plane, _, chip, core = whereabouts()
    copies = Copies(sems)
    for hop in range(CHIPS):
        for flip in range(2):
            copies.start(
                piece_refs[hop].at[pl.ds(flip * plan.piece, plan.piece)], pieces.at[2 * (chip ^ hop) + (core ^ flip)]
            )
    for place, ref in enumerate(halo_refs):
        copies.start(ref, halo_pieces.at[place])

    for group in range(plan.lanes):
        edge = jnp.zeros((plan.window, plan.pad, 128), f32)
        spread[group, 0:plan.window, 0:plan.pad] = edge
        spread[group, 0:plan.window, plan.pad + plan.sub_rows:plan.tall] = edge
        spread[group, plan.window] = jnp.zeros((plan.tall, 128), f32)

    low_rows = iota((8, 128), 0) < 4

    def lay(source, place, row):
        @pl.loop(0, plan.piece // 16)
        def _(quad):
            at = pl.multiple_of(quad * 16, 16)
            for group in range(plan.lanes):
                lanes = pl.ds(group * 128, 128)
                upper = source[place, pl.ds(at, 16), lanes].astype(f32)
                lower = source[place + 1, pl.ds(at, 16), lanes].astype(f32)
                for part in range(2):
                    a, b = upper[8 * part:8 * part + 8], lower[8 * part:8 * part + 8]
                    column = quad * 4 + 2 * part
                    spread[group, column, row:row + 8] = jnp.where(low_rows, a, pltpu.roll(b, 4, 0))
                    spread[group, column + 1, row:row + 8] = jnp.where(low_rows, pltpu.roll(a, 4, 0), b)

    copies.wait()
    for pair in range(CHIPS):
        lay(pieces, 2 * pair, plan.pad + 8 * pair)
    if halo:
        for pair in range(2):
            lay(halo_pieces.at[0], 2 * pair, plan.pad - 16 + 8 * pair)
            lay(halo_pieces.at[1], 2 * pair, plan.pad + plan.sub_rows + 8 * pair)

    segments = plan.segments(plane * CHIPS + chip)
    for branch in range(plan.branches):
        @pl.when(mask_ref[branch] > 0)
        def _():
            shares = [
                tiles_ref[strip * plan.branches + branch].astype(f32)
                for strip in range(-(-9 * plan.lanes // plan.depth_rows))
            ]
            for group in range(plan.lanes):
                kernel = []
                for tap in range(9):
                    row = tap * plan.lanes + group
                    at = plan.tile + row % plan.depth_rows
                    kernel.append(jnp.broadcast_to(shares[row // plan.depth_rows][at:at + 1], (plan.sub_rows, 128)))

                @pl.loop(0, plan.work)
                def _(w):
                    total = None
                    for j in range(3):
                        column = plan.neighbour(segments, w, (j - 1) * (branch + 1))
                        for i in range(3):
                            row = plan.pad + (i - 1) * plan.step_rows * (branch + 1)
                            term = spread[group, column, row:row + plan.sub_rows] * kernel[3 * i + j]
                            total = term if total is None else total + term
                    at = pl.multiple_of(w * plan.sub_rows, plan.sub_rows)
                    dw_out[branch, pl.ds(at, plan.sub_rows), group * 128:(group + 1) * 128] = total.astype(bf16)

    pixel = iota((plan.pixels, 128), 0)
    column = pixel // plan.sub_rows
    row = pixel - column * plan.sub_rows
    source = (row // 2) * plan.tile + 2 * column + row % 2
    lane = iota(source.shape, 1)
    order = jnp.concatenate([one_hot(source == lane + 128 * k) for k in range(plan.pixels // 128)], 1)
    for pair in range(GROUP):
        for couple in range(plan.branches // 2):
            left = tiles_ref[pair * plan.branches + 2 * couple].astype(f32)[:plan.tile]
            right = tiles_ref[pair * plan.branches + 2 * couple + 1].astype(f32)[:plan.tile]
            first, second = swap_halves(left, right)
            lanes = pl.ds(couple * 128, 128)
            sorted_rows[pl.ds(2 * pair * plan.tile, plan.tile), lanes] = first
            sorted_rows[pl.ds((2 * pair + 1) * plan.tile, plan.tile), lanes] = second
    cotangent_ref[...] = dot(order, sorted_rows[...].astype(bf16))
    order_ref[...] = order


def depthwise(plan, mask, tiles, pieces, halos):
    operands = [mask, tiles, *pieces, *halos]
    return pl.pallas_call(
        functools.partial(depthwise_kernel, plan, len(halos) > 0),
        out_shape=[
            jax.ShapeDtypeStruct((plan.branches, plan.pixels, plan.chans), bf16),
            jax.ShapeDtypeStruct((plan.lanes, plan.window + 1, plan.tall, 128), f32),
            jax.ShapeDtypeStruct((plan.pixels, plan.width), f32),
            jax.ShapeDtypeStruct((plan.pixels, plan.pixels), bf16),
            jax.ShapeDtypeStruct((8, 128), f32),
        ],
        in_specs=[SMEM, VMEM] + [ANY] * (len(operands) - 2),
        out_specs=[VMEM] * 5,
        scratch_shapes=[
            pltpu.VMEM((GROUP, plan.piece, plan.chans), bf16),
            pltpu.VMEM((2, 4, plan.piece, plan.chans) if halos else (16, 128), bf16),
            pltpu.VMEM((plan.pixels, plan.width), f32),
            pltpu.SemaphoreType.DMA((GROUP + 2,)),
        ],
        compiler_params=pltpu.CompilerParams(vmem_limit_bytes=20 << 20),
        cost_estimate=pl.CostEstimate(flops=DEPTHWISE_COST, bytes_accessed=1 << 10, transcendentals=0),
        name="depthwise",
    )(*operands)


def main_kernel(plan, scale, mask_ref, dw_out, cotangent_ref, order_ref, *refs):
    branches, width, chans = plan.branches, plan.width, plan.chans
    (point_ref, joining_ref), refs = refs[:2], refs[2:]
    mine_refs, refs = refs[:branches - 1], refs[branches - 1:]
    other_refs, refs = refs[:branches - 1], refs[branches:]
    output_ref, keep_ref, send_ref, grad_pre_ref, point, joining, branch_out, slope, joined, sorted_rows, sems = refs
    plane, _, _, core = whereabouts()
    slots, active_count = slots_of(mask_ref, branches)
    half_point, half_join = chans // 2, width // 2

    def fetches(hop):
        ends = []
        if hop == 0:
            ends = [(point_ref.at[0], point.at[plane]), (joining_ref, joining.at[plane])]
        else:
            for side, ref in ((core, mine_refs[hop - 1]), (1 - core, other_refs[hop - 1])):
                at_point = pl.ds(pl.multiple_of(side * half_point, half_point), half_point)
                at_join = pl.ds(pl.multiple_of(side * half_join, half_join), half_join)
                ends.append((ref.at[pl.ds(0, half_point)], point.at[plane ^ hop, at_point]))
                ends.append((ref.at[pl.ds(half_point, half_join)], joining.at[plane ^ hop, at_join]))
        return [pltpu.make_async_copy(*pair, sems.at[hop, place]) for place, pair in enumerate(ends)]

    for hop in range(branches):
        @pl.when(mask_ref[plane ^ hop] > 0)
        def _():
            for copy in fetches(hop):
                copy.start()

    joined[...] = jnp.zeros_like(joined)
    for hop in range(branches):
        branch = plane ^ hop

        @pl.when(mask_ref[branch] > 0)
        def _():
            for copy in fetches(hop):
                copy.wait()
            value, derivative = gelu_both(dot(dw_out[branch], point[branch]))
            value = value.astype(bf16)
            branch_out[branch] = value
            slope[branch] = derivative
            joined[...] += dot(value, joining[branch])

    value, derivative = gelu_both(joined[...])
    grad_joined = (cotangent_ref[...] * derivative).astype(bf16)

    def store_grads(slot, part, first, rows):
        at = pl.multiple_of(slot * plan.grad_rows + first, 32)
        for half in range(2):
            for kept, ref in ((True, keep_ref), (False, send_ref)):
                @pl.when((core == half) == kept)
                def _():
                    for chip in range(CHIPS):
                        chunk = half * CHIPS + chip
                        ref[chip, pl.ds(at, rows)] = part[chunk * rows:(chunk + 1) * rows]

    @pl.loop(0, branches)
    def _(branch):
        @pl.when(mask_ref[branch] > 0)
        def _():
            slot = pick(slots, branch)
            joining_part = (dot(branch_out[branch], grad_joined, ((0,), (0,))) * scale).astype(bf16)
            store_grads(slot, joining_part, 0, plan.join_rows)
            grad_branch = dot(grad_joined, joining[branch], ((1,), (1,)))
            grad_pre = (grad_branch * slope[branch]).astype(bf16)
            grad_pre_ref[branch] = grad_pre
            point_part = (dot(dw_out[branch], grad_pre, ((0,), (0,))) * scale).astype(bf16)
            store_grads(slot, point_part, plan.join_rows, plan.point_rows)

    for slot in range(1, SLOTS):
        @pl.when(slot >= active_count)
        def _():
            rows = pl.ds(slot * plan.grad_rows, plan.grad_rows)
            empty = jnp.zeros((plan.grad_rows, width), bf16)
            for chip in range(CHIPS):
                keep_ref[chip, rows] = empty
                send_ref[chip, rows] = empty

    sorted_rows[...] = dot(order_ref[...], value.astype(bf16), ((0,), (0,)))
    for pair in range(GROUP):
        for couple in range(branches // 2):
            lanes = pl.ds(couple * 128, 128)
            left = sorted_rows[pl.ds(2 * pair * plan.tile, plan.tile), lanes]
            right = sorted_rows[pl.ds((2 * pair + 1) * plan.tile, plan.tile), lanes]
            first, second = swap_halves(left, right)
            output_ref[pair * branches + 2 * couple] = first.astype(bf16)
            output_ref[pair * branches + 2 * couple + 1] = second.astype(bf16)


def main_step(plan, scale, mask, dw_out, cotangent, order, point, joining, mine, others, token):
    operands = [mask, dw_out, cotangent, order, point, joining, *mine, *others, token]
    half = jax.ShapeDtypeStruct((GROUP // 2, SLOTS * plan.grad_rows, plan.width), bf16)
    return pl.pallas_call(
        functools.partial(main_kernel, plan, scale),
        out_shape=[
            jax.ShapeDtypeStruct((GROUP * plan.branches, plan.tile, 128), bf16),
            half,
            half,
            jax.ShapeDtypeStruct((plan.branches, plan.pixels, plan.width), bf16),
            jax.ShapeDtypeStruct((plan.branches, plan.chans, plan.width), bf16),
        ],
        in_specs=[SMEM] + [VMEM] * 3 + [ANY] * (len(operands) - 4),
        out_specs=[VMEM] * 5,
        scratch_shapes=[
            pltpu.VMEM((plan.branches, plan.width, plan.width), bf16),
            pltpu.VMEM((plan.branches, plan.pixels, plan.width), bf16),
            pltpu.VMEM((plan.branches, plan.pixels, plan.width), f32),
            pltpu.VMEM((plan.pixels, plan.width), f32),
            pltpu.VMEM((plan.pixels, plan.width), f32),
            pltpu.SemaphoreType.DMA((plan.branches, 4)),
        ],
        compiler_params=pltpu.CompilerParams(vmem_limit_bytes=24 << 20),
        cost_estimate=pl.CostEstimate(flops=1 << 31, bytes_accessed=1 << 24, transcendentals=0),
        name="forward_and_backward",
    )(*operands)


def depth_grad_kernel(plan, scale, mask_ref, grad_pre_ref, point, spread, out_ref, grad_dw, rows):
    plane, _, chip, _ = whereabouts()
    slots, _ = slots_of(mask_ref, plan.branches)
    segments = plan.segments(plane * CHIPS + chip)
    out_ref[...] = jnp.zeros_like(out_ref)
    rows[...] = jnp.zeros_like(rows)
    for branch in range(plan.branches):
        @pl.when(mask_ref[branch] > 0)
        def _():
            grad_pre = grad_pre_ref[branch]
            for group in range(plan.lanes):
                grad_dw[group] = dot(grad_pre, point[branch, group * 128:(group + 1) * 128], ((1,), (1,)))
            for group in range(plan.lanes):
                def add_column(w, sums):
                    at = pl.multiple_of(w * plan.sub_rows, plan.sub_rows)
                    given = grad_dw[group, pl.ds(at, plan.sub_rows)]
                    sums = list(sums)
                    for j in range(3):
                        column = plan.neighbour(segments, w, (j - 1) * (branch + 1))
                        for i in range(3):
                            row = plan.pad + (i - 1) * plan.step_rows * (branch + 1)
                            product = spread[group, column, row:row + plan.sub_rows] * given
                            for part in range(plan.sub_rows // 8):
                                sums[3 * i + j] = sums[3 * i + j] + product[8 * part:8 * part + 8]
                    return tuple(sums)

                sums = lax.fori_loop(0, plan.work, add_column, (jnp.zeros((8, 128), f32),) * 9)
                lanes = slice((group % 2) * 128, (group % 2) * 128 + 128)
                for tap in range(9):
                    row = 2 * tap + group // 2
                    rows[row:row + 1, lanes] = jnp.sum(sums[tap], axis=0, keepdims=True) * scale
            out_ref[slots[branch]] = rows[...].astype(bf16)


def depth_grad(plan, scale, mask, grad_pre, point, spread):
    return pl.pallas_call(
        functools.partial(depth_grad_kernel, plan, scale),
        out_shape=jax.ShapeDtypeStruct((SLOTS, 32, plan.width), bf16),
        in_specs=[SMEM] + [VMEM] * 3,
        out_specs=VMEM,
        scratch_shapes=[
            pltpu.VMEM((plan.lanes, plan.pixels, 128), f32),
            pltpu.VMEM((32, plan.width), f32),
        ],
        compiler_params=pltpu.CompilerParams(vmem_limit_bytes=24 << 20),
        cost_estimate=pl.CostEstimate(flops=1 << 26, bytes_accessed=1 << 24, transcendentals=0),
        name="depth_grad",
    )(mask, grad_pre, point, spread)


def chip_sum_kernel(keep_ref, other_ref, *out_refs):
    _, _, chip, _ = whereabouts()
    for hop in range(CHIPS):
        out_refs[hop][...] = (keep_ref[chip ^ hop].astype(f32) + other_ref[chip ^ hop].astype(f32)).astype(bf16)


def chip_sum(keep, other):
    return pl.pallas_call(
        chip_sum_kernel,
        out_shape=[jax.ShapeDtypeStruct(keep.shape[1:], bf16)] * CHIPS,
        in_specs=[VMEM] * 2,
        out_specs=[VMEM] * CHIPS,
        compiler_params=pltpu.CompilerParams(vmem_limit_bytes=16 << 20),
        name="chip_sum",
    )(keep, other)


def plane_sum_kernel(plan, mask_ref, depth_ref, *refs):
    total, out_refs = refs[-1], refs[CHIPS:-1]
    plane, _, _, _ = whereabouts()
    slots, _ = slots_of(mask_ref, plan.branches)
    added = refs[0][...].astype(f32)
    for ref in refs[1:CHIPS]:
        added = added + ref[...].astype(f32)
    total[...] = added
    rows = plan.grad_rows
    for hop in range(plan.branches):
        slot = pick(slots, plane ^ hop)
        out_refs[hop][0:rows] = total[pl.ds(pl.multiple_of(slot * rows, 32), rows)].astype(bf16)
        out_refs[hop][rows:] = depth_ref[slot]


def plane_sum(plan, mask, depth, parts):
    return pl.pallas_call(
        functools.partial(plane_sum_kernel, plan),
        out_shape=[jax.ShapeDtypeStruct((plan.grad_rows + depth.shape[1], plan.width), bf16)] * plan.branches,
        in_specs=[SMEM] + [VMEM] * (1 + CHIPS),
        out_specs=[VMEM] * plan.branches,
        scratch_shapes=[pltpu.VMEM(parts[0].shape, f32)],
        compiler_params=pltpu.CompilerParams(vmem_limit_bytes=16 << 20),
        name="plane_sum",
    )(mask, depth, *parts)


def place_grads_kernel(plan, mask_ref, *refs):
    chunk_refs, (joining_ref, point_ref, depth_ref) = refs[:GROUP], refs[GROUP + 1:]
    plane, _, chip, core = whereabouts()
    active = pick([mask_ref[branch] for branch in range(plan.branches)], plane) > 0
    rows = plan.grad_rows
    taps = None
    for flip in range(2):
        for hop in range(CHIPS):
            chunk = jnp.where(active, chunk_refs[flip * CHIPS + hop][...].astype(f32), 0.0)
            at = (core ^ flip) * CHIPS + (chip ^ hop)
            joining_ref[pl.ds(pl.multiple_of(at * plan.join_rows, plan.join_rows), plan.join_rows)] = chunk[:plan.join_rows]
            place = pl.multiple_of(at * plan.point_rows, plan.point_rows)
            point_ref[0, pl.ds(place, plan.point_rows)] = chunk[plan.join_rows:rows]
            taps = chunk[rows:] if taps is None else taps + chunk[rows:]
    for tap in range(9):
        for group in range(plan.lanes):
            row, lane = 2 * tap + group // 2, (group % 2) * 128
            depth_ref[0, tap:tap + 1, group * 128:(group + 1) * 128] = taps[row:row + 1, lane:lane + 128]


def place_grads(plan, mask, chunks, token):
    return pl.pallas_call(
        functools.partial(place_grads_kernel, plan),
        out_shape=[
            jax.ShapeDtypeStruct((plan.width, plan.width), f32),
            jax.ShapeDtypeStruct((1, plan.chans, plan.width), f32),
            jax.ShapeDtypeStruct((1, 9, plan.chans), f32),
        ],
        in_specs=[SMEM] + [VMEM] * GROUP + [ANY],
        out_specs=[VMEM] * 3,
        compiler_params=pltpu.CompilerParams(vmem_limit_bytes=16 << 20),
        name="place_grads",
    )(mask, *chunks, token)


def per_device(features, cotangent, depth_weight, point_weight, joining_weight, branch_mask):
    row_count, col_count, chan_count = features.shape
    strips = lax.axis_size("strip")
    branches = lax.axis_size("branch")
    width = joining_weight.shape[1]
    plan = Plan(row_count, col_count, chan_count, width, branches)
    scale = 1.0 / math.sqrt(row_count * col_count * strips)
    groups = None if strips == GROUP else [list(range(g, g + GROUP)) for g in range(0, strips, GROUP)]

    def flip_strip(value, hop):
        return lax.ppermute(value, "strip", [(s, s ^ hop) for s in range(strips)])

    def flip_branch(value, hop):
        return lax.ppermute(value, "branch", [(b, b ^ hop) for b in range(branches)])

    def all_to_all(tiles):
        if groups is None:
            return lax.all_to_all(tiles, ("strip", "branch"), 0, 0, tiled=True)
        tiles = tiles.reshape(GROUP, branches, *tiles.shape[1:])
        tiles = lax.all_to_all(tiles, "branch", 1, 1, tiled=True)
        tiles = lax.all_to_all(tiles, "strip", 0, 0, tiled=True, axis_index_groups=groups)
        return tiles.reshape(GROUP * branches, *tiles.shape[2:])

    half = halve_weights(plan, point_weight, joining_weight)
    mine = [flip_branch(half, 1), flip_branch(half, 2)]
    mine.append(flip_branch(mine[1], 1))

    keep, send = spread_features(plan, features)
    joint = join_features(plan, keep, flip_strip(send, 1))
    pieces = [joint[0]] + [flip_strip(joint[hop], 2 * hop) for hop in range(1, CHIPS)]
    halos = []
    if groups is not None:
        strip = lax.axis_index("strip") % GROUP
        near = jnp.stack(pieces).reshape(CHIPS, 2, plan.piece, plan.chans)
        at = jnp.arange(GROUP)
        near = near[(at // 2) ^ (strip // 2), (at % 2) ^ (strip % 2)]
        down = [(s, s + GROUP) for s in range(strips - GROUP)]
        up = [(s + GROUP, s) for s in range(strips - GROUP)]
        halos = [lax.ppermute(near[GROUP - 4:], "strip", down), lax.ppermute(near[:4], "strip", up)]
    tiles = all_to_all(send_cotangent(plan, jnp.swapaxes(cotangent, 1, 2), depth_weight))
    dw_out, spread, pixel_cotangent, order, token = depthwise(plan, branch_mask, tiles, pieces, halos)

    mine, token = lax.optimization_barrier((mine, token))
    others = [flip_strip(value, 1) for value in mine]
    output_tiles, keep, send, grad_pre, points = main_step(
        plan, scale, branch_mask, dw_out, pixel_cotangent, order, point_weight, joining_weight, mine, others, token
    )
    parts = chip_sum(keep, flip_strip(send, 1))
    parts, output_tiles, grad_pre = lax.optimization_barrier((parts, output_tiles, grad_pre))
    parts = [parts[0]] + [flip_strip(parts[hop], 2 * hop) for hop in range(1, CHIPS)]
    taps = depth_grad(plan, scale, branch_mask, grad_pre, points, spread)
    output, token = place_output(plan, all_to_all(output_tiles))
    shares = plane_sum(plan, branch_mask, taps, parts)
    shares = [shares[0]] + [flip_branch(shares[hop], hop) for hop in range(1, branches)]
    share = sum(value.astype(f32) for value in shares)
    if groups is not None:
        peers = [list(range(s, strips, GROUP)) for s in range(GROUP)]
        share = lax.psum(share, "strip", axis_index_groups=peers)
    share = share.astype(bf16)
    chunks = [share] + [flip_strip(share, 2 * hop) for hop in range(1, CHIPS)]
    chunks = chunks + [flip_strip(chunk, 1) for chunk in chunks]
    joining_total, point_total, depth_total = place_grads(plan, branch_mask, chunks, token)
    return (jnp.swapaxes(output, 1, 2), joining_total, point_total, depth_total)


def solution(mesh):
    placed = (
        P("strip", None, None),
        P("strip", None, "branch"),
        P("branch", None, None),
        P("branch", None, None),
        P("branch", None),
        P(),
    )
    return jax.shard_map(
        per_device,
        mesh=mesh,
        in_specs=placed,
        out_specs=(
            P("strip", None, "branch"),
            P("branch", None),
            P("branch", None, None),
            P("branch", None, None),
        ),
        check_vma=False,
    )
```

```python
import functools
import math

import jax
import jax.numpy as jnp
from jax import lax
from jax.experimental import pallas as pl
from jax.experimental.pallas import tpu as pltpu
from jax.sharding import PartitionSpec as P

DILATION_STEP = 6
GROUP = 8
CHIPS = 4
DEPTHWISE_COST = 1 << 31
SLOTS = 3

tanh_coef = 0.7978845608
cubic_coef = 0.044715
slope_coef = 0.134145

f32, bf16, i32 = jnp.float32, jnp.bfloat16, jnp.int32
VMEM = pl.BlockSpec(memory_space=pltpu.VMEM)
SMEM = pl.BlockSpec(memory_space=pltpu.SMEM)
ANY = pl.BlockSpec(memory_space=pl.ANY)
HBM = pl.BlockSpec(memory_space=pltpu.HBM)


def gelu_both(values):
    square = values * values
    inner = jnp.tanh(tanh_coef * (values + cubic_coef * values * square))
    half = 0.5 * (1.0 + inner)
    slope = half + 0.5 * values * (1.0 - inner * inner) * tanh_coef * (1.0 + slope_coef * square)
    return values * half, slope


def dot(left, right, dims=((1,), (0,))):
    return lax.dot_general(left, right, (dims, ((), ())), preferred_element_type=f32)


def iota(shape, dim):
    return lax.broadcasted_iota(i32, shape, dim)


def one_hot(mask):
    return jnp.where(mask, 1.0, 0.0).astype(bf16)


class Plan:
    def __init__(self, row_count, col_count, chan_count, width, branches):
        self.rows, self.cols, self.chans, self.width, self.branches = row_count, col_count, chan_count, width, branches
        self.classes = DILATION_STEP
        self.run = col_count // DILATION_STEP
        self.work = col_count // (branches * CHIPS)
        self.taps_t = row_count // 2
        self.sub_rows = GROUP * self.taps_t
        self.pixels = self.sub_rows * self.work
        self.lanes = chan_count // 128
        self.window = max(self.segments(m)[5] for m in range(branches * CHIPS))
        self.piece = self.window * self.taps_t
        self.part = width // branches
        self.step_rows = DILATION_STEP // 2
        self.pad = -(-self.step_rows * branches // 16) * 16
        self.tall = self.pad + self.sub_rows + self.pad
        self.grad_rows = (width + chan_count) // GROUP
        self.join_rows = width // GROUP
        self.point_rows = chan_count // GROUP
        self.tile = 2 * self.work
        self.depth_rows = -(-9 * self.lanes // GROUP // 8) * 8
        self.wide = -(-self.cols // 128) * 128

    def segments(self, m):
        smaller, larger = (min, max) if isinstance(m, int) else (jnp.minimum, jnp.maximum)
        first = m * self.work
        klass = first // self.run
        start = first - klass * self.run
        length = smaller(self.work, self.run - start)
        low = larger(0, start - self.branches)
        size = smaller(self.run, start + length + self.branches) - low
        rest = self.work - length
        if isinstance(m, int):
            total = size + (min(self.run, rest + self.branches) if rest else 0)
        else:
            total = size + jnp.where(rest > 0, jnp.minimum(self.run, rest + self.branches), 0)
        return klass, start, length, low, size, total

    def column(self, m, w):
        klass, start, length, _, _, _ = self.segments(m)
        return jnp.where(w < length, self.classes * (start + w) + klass, self.classes * (w - length) + klass + 1)

    def window_column(self, m, j):
        klass, _, _, low, size, total = self.segments(m)
        inside = jnp.where(j < size, self.classes * (low + j) + klass, self.classes * (j - size) + klass + 1)
        return jnp.where(j < total, inside, -(1 << 20))

    def neighbour(self, segments, w, shift):
        _, start, length, low, size, _ = segments
        first = w < length
        place = jnp.where(first, start + w, w - length) + shift
        found = jnp.where(first, place - low, size + place)
        return jnp.where(jnp.logical_and(place >= 0, place < self.run), found, self.window)


def whereabouts():
    strip = lax.axis_index("strip") % GROUP
    return lax.axis_index("branch"), strip, strip // 2, strip % 2


def slots_of(mask_ref, branches):
    slots, count = [], 0
    for branch in range(branches):
        slots.append(jnp.minimum(count, SLOTS - 1) + 0 * mask_ref[branch])
        count = count + mask_ref[branch]
    return slots, count


def pick(values, index):
    result = values[0]
    for place in range(1, len(values)):
        result = jnp.where(index == place, values[place], result)
    return result


def tile_selector(plan):
    blocks = []
    for chip in range(CHIPS):
        for plane in range(plan.branches):
            row = iota((plan.tile, 128), 0)
            column = plan.column(plane * CHIPS + chip, row // 2)
            blocks.append(column + (row % 2) * plan.wide)
    target = jnp.concatenate(blocks, 0)
    lane = iota(target.shape, 1)
    return jnp.concatenate([one_hot(target == lane + 128 * k) for k in range(2 * plan.wide // 128)], 1)


def halve_kernel(plan, point_ref, joining_ref, half_ref, sems):
    _, _, _, core = whereabouts()
    half_point, half_join = plan.chans // 2, plan.width // 2
    copies = [
        pltpu.make_async_copy(
            point_ref.at[0, pl.ds(pl.multiple_of(core * half_point, half_point), half_point)],
            half_ref.at[pl.ds(0, half_point)],
            sems.at[0],
        ),
        pltpu.make_async_copy(
            joining_ref.at[pl.ds(pl.multiple_of(core * half_join, half_join), half_join)],
            half_ref.at[pl.ds(half_point, half_join)],
            sems.at[1],
        ),
    ]
    for copy in copies:
        copy.start()
    for copy in copies:
        copy.wait()


def halve_weights(plan, point, joining):
    return pl.pallas_call(
        functools.partial(halve_kernel, plan),
        out_shape=jax.ShapeDtypeStruct(((plan.chans + plan.width) // 2, plan.width), bf16),
        in_specs=[HBM] * 2,
        out_specs=VMEM,
        scratch_shapes=[pltpu.SemaphoreType.DMA((2,))],
        compiler_params=pltpu.CompilerParams(vmem_limit_bytes=8 << 20),
        name="halve_weights",
    )(point, joining)


def spread_kernel(plan, features_ref, keep_ref, send_ref):
    plane, _, _, core = whereabouts()
    depth = plan.taps_t * plan.cols
    targets = []
    for chip in range(CHIPS):
        row = iota((plan.piece, 128), 0)
        column = plan.window_column(plane * CHIPS + chip, row // plan.taps_t)
        targets.append(column + (row % plan.taps_t) * plan.cols)
    target = jnp.concatenate(targets, 0)
    lane = iota(target.shape, 1)
    chosen = jnp.concatenate([one_hot(target == lane + 128 * k) for k in range(depth // 128)], 1)
    for flip, out_ref in enumerate((keep_ref, send_ref)):
        rows = jnp.concatenate([features_ref[2 * t + (core ^ flip)] for t in range(plan.taps_t)], 0)
        found = dot(chosen, rows).astype(bf16)
        for chip in range(CHIPS):
            out_ref[chip] = found[chip * plan.piece:(chip + 1) * plan.piece]


def spread_features(plan, features):
    half = jax.ShapeDtypeStruct((CHIPS, plan.piece, plan.chans), bf16)
    return pl.pallas_call(
        functools.partial(spread_kernel, plan),
        out_shape=[half, half],
        in_specs=[VMEM],
        out_specs=[VMEM] * 2,
        compiler_params=pltpu.CompilerParams(vmem_limit_bytes=16 << 20),
        name="spread_features",
    )(features)


def join_kernel(plan, keep_ref, other_ref, *out_refs):
    _, _, chip, _ = whereabouts()
    for hop in range(CHIPS):
        out_refs[hop][0:plan.piece] = keep_ref[chip ^ hop]
        out_refs[hop][plan.piece:] = other_ref[chip ^ hop]


def join_features(plan, keep, other):
    return pl.pallas_call(
        functools.partial(join_kernel, plan),
        out_shape=[jax.ShapeDtypeStruct((2 * plan.piece, plan.chans), bf16)] * CHIPS,
        in_specs=[VMEM] * 2,
        out_specs=[VMEM] * CHIPS,
        compiler_params=pltpu.CompilerParams(vmem_limit_bytes=8 << 20),
        name="join_features",
    )(keep, other)


def send_cotangent_kernel(plan, cotangent_ref, depth_ref, tiles_ref, cotangent, depth, taps, sems):
    _, strip, _, _ = whereabouts()
    copies = [
        pltpu.make_async_copy(cotangent_ref, cotangent, sems.at[0]),
        pltpu.make_async_copy(depth_ref, depth, sems.at[1]),
    ]
    for copy in copies:
        copy.start()
    chosen = tile_selector(plan)
    for copy in copies:
        copy.wait()

    taps[...] = jnp.zeros_like(taps)
    values = depth[0].astype(f32)
    for tap in range(9):
        for group in range(plan.lanes):
            row = tap * plan.lanes + group
            taps[row:row + 1] = values[tap:tap + 1, group * 128:(group + 1) * 128]
    share = taps[pl.ds(pl.multiple_of(strip * plan.depth_rows, 8), plan.depth_rows)]
    fill = jnp.zeros((plan.part, plan.wide - plan.cols), f32)
    blocks = []
    for parity in range(2):
        for high in range(2):
            rows = []
            for low in range(2):
                rows += [cotangent[2 * (2 * high + low) + parity].astype(f32), fill]
            blocks.append(jnp.concatenate(rows, 1))
    found = dot(chosen, jnp.concatenate(blocks, 0).astype(bf16), ((1,), (1,)))
    for chip in range(CHIPS):
        for parity in range(2):
            for plane in range(plan.branches):
                at = (chip * plan.branches + plane) * plan.tile
                tile = found[at:at + plan.tile, parity * 128:(parity + 1) * 128]
                tiles_ref[(2 * chip + parity) * plan.branches + plane] = jnp.concatenate([tile, share], 0).astype(bf16)


def send_cotangent(plan, cotangent, depth):
    return pl.pallas_call(
        functools.partial(send_cotangent_kernel, plan),
        out_shape=jax.ShapeDtypeStruct((GROUP * plan.branches, plan.tile + plan.depth_rows, 128), bf16),
        in_specs=[HBM] * 2,
        out_specs=VMEM,
        scratch_shapes=[
            pltpu.VMEM(cotangent.shape, bf16),
            pltpu.VMEM(depth.shape, bf16),
            pltpu.VMEM((GROUP * plan.depth_rows, 128), f32),
            pltpu.SemaphoreType.DMA((2,)),
        ],
        compiler_params=pltpu.CompilerParams(vmem_limit_bytes=60 << 20),
        cost_estimate=pl.CostEstimate(flops=1, bytes_accessed=1, transcendentals=0),
        name="send_cotangent",
    )(cotangent, depth)


def place_output_kernel(plan, tiles_ref, out_ref, token_ref):
    token_ref[...] = jnp.zeros_like(token_ref)
    chosen = tile_selector(plan)
    halves = []
    for parity in range(2):
        blocks = []
        for chip in range(CHIPS):
            for plane in range(plan.branches):
                blocks.append(tiles_ref[(2 * chip + parity) * plan.branches + plane].astype(f32))
        halves.append(jnp.concatenate(blocks, 0))
    found = dot(jnp.concatenate(halves, 1).astype(bf16), chosen, ((0,), (0,))).astype(bf16)
    for parity in range(2):
        for high in range(2):
            for low in range(2):
                at = parity * 128 + high * plan.part
                out_ref[2 * (2 * high + low) + parity] = found[
                    at:at + plan.part, low * plan.wide:low * plan.wide + plan.cols
                ]


def place_output(plan, tiles):
    return pl.pallas_call(
        functools.partial(place_output_kernel, plan),
        out_shape=[
            jax.ShapeDtypeStruct((plan.rows, plan.part, plan.cols), bf16),
            jax.ShapeDtypeStruct((8, 128), f32),
        ],
        in_specs=[VMEM],
        out_specs=[VMEM] * 2,
        compiler_params=pltpu.CompilerParams(vmem_limit_bytes=16 << 20),
        name="place_output",
    )(tiles)


def swap_halves(left, right):
    low = iota(left.shape, 1) < 64
    return (
        jnp.where(low, left, pltpu.roll(right, 64, 1)),
        jnp.where(low, pltpu.roll(left, 64, 1), right),
    )


class Copies:
    def __init__(self, sems):
        self.sems, self.all = sems, []

    def start(self, source, target):
        copy = pltpu.make_async_copy(source, target, self.sems.at[len(self.all)])
        copy.start()
        self.all.append(copy)

    def wait(self):
        for copy in self.all:
            copy.wait()
        self.all = []


def depthwise_kernel(plan, halo, mask_ref, tiles_ref, *refs):
    piece_refs, refs = refs[:CHIPS], refs[CHIPS:]
    halo_refs, refs = (refs[:2], refs[2:]) if halo else ((), refs)
    dw_out, spread, cotangent_ref, order_ref, token, pieces, halo_pieces, sorted_rows, sems = refs
    token[...] = jnp.zeros_like(token)
    plane, _, chip, core = whereabouts()
    copies = Copies(sems)
    for hop in range(CHIPS):
        for flip in range(2):
            copies.start(
                piece_refs[hop].at[pl.ds(flip * plan.piece, plan.piece)], pieces.at[2 * (chip ^ hop) + (core ^ flip)]
            )
    for place, ref in enumerate(halo_refs):
        copies.start(ref, halo_pieces.at[place])

    for group in range(plan.lanes):
        edge = jnp.zeros((plan.window, plan.pad, 128), f32)
        spread[group, 0:plan.window, 0:plan.pad] = edge
        spread[group, 0:plan.window, plan.pad + plan.sub_rows:plan.tall] = edge
        spread[group, plan.window] = jnp.zeros((plan.tall, 128), f32)

    low_rows = iota((8, 128), 0) < 4

    def lay(source, place, row):
        @pl.loop(0, plan.piece // 16)
        def _(quad):
            at = pl.multiple_of(quad * 16, 16)
            for group in range(plan.lanes):
                lanes = pl.ds(group * 128, 128)
                upper = source[place, pl.ds(at, 16), lanes].astype(f32)
                lower = source[place + 1, pl.ds(at, 16), lanes].astype(f32)
                for part in range(2):
                    a, b = upper[8 * part:8 * part + 8], lower[8 * part:8 * part + 8]
                    column = quad * 4 + 2 * part
                    spread[group, column, row:row + 8] = jnp.where(low_rows, a, pltpu.roll(b, 4, 0))
                    spread[group, column + 1, row:row + 8] = jnp.where(low_rows, pltpu.roll(a, 4, 0), b)

    copies.wait()
    for pair in range(CHIPS):
        lay(pieces, 2 * pair, plan.pad + 8 * pair)
    if halo:
        for pair in range(2):
            lay(halo_pieces.at[0], 2 * pair, plan.pad - 16 + 8 * pair)
            lay(halo_pieces.at[1], 2 * pair, plan.pad + plan.sub_rows + 8 * pair)

    segments = plan.segments(plane * CHIPS + chip)
    for branch in range(plan.branches):
        @pl.when(mask_ref[branch] > 0)
        def _():
            shares = [
                tiles_ref[strip * plan.branches + branch].astype(f32)
                for strip in range(-(-9 * plan.lanes // plan.depth_rows))
            ]
            for group in range(plan.lanes):
                kernel = []
                for tap in range(9):
                    row = tap * plan.lanes + group
                    at = plan.tile + row % plan.depth_rows
                    kernel.append(jnp.broadcast_to(shares[row // plan.depth_rows][at:at + 1], (plan.sub_rows, 128)))

                @pl.loop(0, plan.work)
                def _(w):
                    total = None
                    for j in range(3):
                        column = plan.neighbour(segments, w, (j - 1) * (branch + 1))
                        for i in range(3):
                            row = plan.pad + (i - 1) * plan.step_rows * (branch + 1)
                            term = spread[group, column, row:row + plan.sub_rows] * kernel[3 * i + j]
                            total = term if total is None else total + term
                    at = pl.multiple_of(w * plan.sub_rows, plan.sub_rows)
                    dw_out[branch, pl.ds(at, plan.sub_rows), group * 128:(group + 1) * 128] = total.astype(bf16)

    pixel = iota((plan.pixels, 128), 0)
    column = pixel // plan.sub_rows
    row = pixel - column * plan.sub_rows
    source = (row // 2) * plan.tile + 2 * column + row % 2
    lane = iota(source.shape, 1)
    order = jnp.concatenate([one_hot(source == lane + 128 * k) for k in range(plan.pixels // 128)], 1)
    for pair in range(GROUP):
        for couple in range(plan.branches // 2):
            left = tiles_ref[pair * plan.branches + 2 * couple].astype(f32)[:plan.tile]
            right = tiles_ref[pair * plan.branches + 2 * couple + 1].astype(f32)[:plan.tile]
            first, second = swap_halves(left, right)
            lanes = pl.ds(couple * 128, 128)
            sorted_rows[pl.ds(2 * pair * plan.tile, plan.tile), lanes] = first
            sorted_rows[pl.ds((2 * pair + 1) * plan.tile, plan.tile), lanes] = second
    cotangent_ref[...] = dot(order, sorted_rows[...].astype(bf16))
    order_ref[...] = order


def depthwise(plan, mask, tiles, pieces, halos):
    operands = [mask, tiles, *pieces, *halos]
    return pl.pallas_call(
        functools.partial(depthwise_kernel, plan, len(halos) > 0),
        out_shape=[
            jax.ShapeDtypeStruct((plan.branches, plan.pixels, plan.chans), bf16),
            jax.ShapeDtypeStruct((plan.lanes, plan.window + 1, plan.tall, 128), f32),
            jax.ShapeDtypeStruct((plan.pixels, plan.width), f32),
            jax.ShapeDtypeStruct((plan.pixels, plan.pixels), bf16),
            jax.ShapeDtypeStruct((8, 128), f32),
        ],
        in_specs=[SMEM, VMEM] + [ANY] * (len(operands) - 2),
        out_specs=[VMEM] * 5,
        scratch_shapes=[
            pltpu.VMEM((GROUP, plan.piece, plan.chans), bf16),
            pltpu.VMEM((2, 4, plan.piece, plan.chans) if halos else (16, 128), bf16),
            pltpu.VMEM((plan.pixels, plan.width), f32),
            pltpu.SemaphoreType.DMA((GROUP + 2,)),
        ],
        compiler_params=pltpu.CompilerParams(vmem_limit_bytes=20 << 20),
        cost_estimate=pl.CostEstimate(flops=DEPTHWISE_COST, bytes_accessed=1 << 10, transcendentals=0),
        name="depthwise",
    )(*operands)


def main_kernel(plan, scale, mask_ref, dw_out, cotangent_ref, *refs):
    branches, width, chans = plan.branches, plan.width, plan.chans
    (point_ref, joining_ref), refs = refs[:2], refs[2:]
    mine_refs, refs = refs[:branches - 1], refs[branches - 1:]
    other_refs, refs = refs[:branches - 1], refs[branches:]
    value_ref, keep_ref, send_ref, grad_pre_ref, point, joining, branch_out, slope, joined, sems = refs
    plane, _, _, core = whereabouts()
    slots, active_count = slots_of(mask_ref, branches)
    half_point, half_join = chans // 2, width // 2

    def fetches(hop):
        ends = []
        if hop == 0:
            ends = [(point_ref.at[0], point.at[plane]), (joining_ref, joining.at[plane])]
        else:
            for side, ref in ((core, mine_refs[hop - 1]), (1 - core, other_refs[hop - 1])):
                at_point = pl.ds(pl.multiple_of(side * half_point, half_point), half_point)
                at_join = pl.ds(pl.multiple_of(side * half_join, half_join), half_join)
                ends.append((ref.at[pl.ds(0, half_point)], point.at[plane ^ hop, at_point]))
                ends.append((ref.at[pl.ds(half_point, half_join)], joining.at[plane ^ hop, at_join]))
        return [pltpu.make_async_copy(*pair, sems.at[hop, place]) for place, pair in enumerate(ends)]

    for hop in range(branches):
        @pl.when(mask_ref[plane ^ hop] > 0)
        def _():
            for copy in fetches(hop):
                copy.start()

    joined[...] = jnp.zeros_like(joined)
    for hop in range(branches):
        branch = plane ^ hop

        @pl.when(mask_ref[branch] > 0)
        def _():
            for copy in fetches(hop):
                copy.wait()
            value, derivative = gelu_both(dot(dw_out[branch], point[branch]))
            value = value.astype(bf16)
            branch_out[branch] = value
            slope[branch] = derivative
            joined[...] += dot(value, joining[branch])

    value, derivative = gelu_both(joined[...])
    grad_joined = (cotangent_ref[...] * derivative).astype(bf16)

    def store_grads(slot, part, first, rows):
        at = pl.multiple_of(slot * plan.grad_rows + first, 32)
        for half in range(2):
            for kept, ref in ((True, keep_ref), (False, send_ref)):
                @pl.when((core == half) == kept)
                def _():
                    for chip in range(CHIPS):
                        chunk = half * CHIPS + chip
                        ref[chip, pl.ds(at, rows)] = part[chunk * rows:(chunk + 1) * rows]

    @pl.loop(0, branches)
    def _(branch):
        @pl.when(mask_ref[branch] > 0)
        def _():
            slot = pick(slots, branch)
            joining_part = (dot(branch_out[branch], grad_joined, ((0,), (0,))) * scale).astype(bf16)
            store_grads(slot, joining_part, 0, plan.join_rows)
            grad_branch = dot(grad_joined, joining[branch], ((1,), (1,)))
            grad_pre = (grad_branch * slope[branch]).astype(bf16)
            grad_pre_ref[branch] = grad_pre
            point_part = (dot(dw_out[branch], grad_pre, ((0,), (0,))) * scale).astype(bf16)
            store_grads(slot, point_part, plan.join_rows, plan.point_rows)

    for slot in range(1, SLOTS):
        @pl.when(slot >= active_count)
        def _():
            rows = pl.ds(slot * plan.grad_rows, plan.grad_rows)
            empty = jnp.zeros((plan.grad_rows, width), bf16)
            for chip in range(CHIPS):
                keep_ref[chip, rows] = empty
                send_ref[chip, rows] = empty

    value_ref[...] = value.astype(bf16)


def main_step(plan, scale, mask, dw_out, cotangent, point, joining, mine, others, token):
    operands = [mask, dw_out, cotangent, point, joining, *mine, *others, token]
    half = jax.ShapeDtypeStruct((GROUP // 2, SLOTS * plan.grad_rows, plan.width), bf16)
    return pl.pallas_call(
        functools.partial(main_kernel, plan, scale),
        out_shape=[
            jax.ShapeDtypeStruct((plan.pixels, plan.width), bf16),
            half,
            half,
            jax.ShapeDtypeStruct((plan.branches, plan.pixels, plan.width), bf16),
            jax.ShapeDtypeStruct((plan.branches, plan.chans, plan.width), bf16),
        ],
        in_specs=[SMEM] + [VMEM] * 2 + [ANY] * (len(operands) - 3),
        out_specs=[VMEM] * 5,
        scratch_shapes=[
            pltpu.VMEM((plan.branches, plan.width, plan.width), bf16),
            pltpu.VMEM((plan.branches, plan.pixels, plan.width), bf16),
            pltpu.VMEM((plan.branches, plan.pixels, plan.width), f32),
            pltpu.VMEM((plan.pixels, plan.width), f32),
            pltpu.SemaphoreType.DMA((plan.branches, 4)),
        ],
        compiler_params=pltpu.CompilerParams(vmem_limit_bytes=24 << 20),
        cost_estimate=pl.CostEstimate(flops=1 << 31, bytes_accessed=1 << 24, transcendentals=0),
        name="forward_and_backward",
    )(*operands)


def depth_grad_kernel(
    plan, scale, mask_ref, grad_pre_ref, point, spread, value_ref, order_ref, out_ref, output_ref, grad_dw, rows, sorted_rows
):
    branches = plan.branches
    sorted_rows[...] = dot(order_ref[...], value_ref[...], ((0,), (0,)))
    for pair in range(GROUP):
        for couple in range(branches // 2):
            lanes = pl.ds(couple * 128, 128)
            left = sorted_rows[pl.ds(2 * pair * plan.tile, plan.tile), lanes]
            right = sorted_rows[pl.ds((2 * pair + 1) * plan.tile, plan.tile), lanes]
            first, second = swap_halves(left, right)
            output_ref[pair * branches + 2 * couple] = first.astype(bf16)
            output_ref[pair * branches + 2 * couple + 1] = second.astype(bf16)
    plane, _, chip, _ = whereabouts()
    slots, _ = slots_of(mask_ref, plan.branches)
    segments = plan.segments(plane * CHIPS + chip)
    out_ref[...] = jnp.zeros_like(out_ref)
    rows[...] = jnp.zeros_like(rows)
    for branch in range(plan.branches):
        @pl.when(mask_ref[branch] > 0)
        def _():
            grad_pre = grad_pre_ref[branch]
            for group in range(plan.lanes):
                grad_dw[group] = dot(grad_pre, point[branch, group * 128:(group + 1) * 128], ((1,), (1,)))
            for group in range(plan.lanes):
                def add_column(w, sums):
                    at = pl.multiple_of(w * plan.sub_rows, plan.sub_rows)
                    given = grad_dw[group, pl.ds(at, plan.sub_rows)]
                    sums = list(sums)
                    for j in range(3):
                        column = plan.neighbour(segments, w, (j - 1) * (branch + 1))
                        for i in range(3):
                            row = plan.pad + (i - 1) * plan.step_rows * (branch + 1)
                            product = spread[group, column, row:row + plan.sub_rows] * given
                            for part in range(plan.sub_rows // 8):
                                sums[3 * i + j] = sums[3 * i + j] + product[8 * part:8 * part + 8]
                    return tuple(sums)

                sums = lax.fori_loop(0, plan.work, add_column, (jnp.zeros((8, 128), f32),) * 9)
                lanes = slice((group % 2) * 128, (group % 2) * 128 + 128)
                for tap in range(9):
                    row = 2 * tap + group // 2
                    rows[row:row + 1, lanes] = jnp.sum(sums[tap], axis=0, keepdims=True) * scale
            out_ref[slots[branch]] = rows[...].astype(bf16)


def depth_grad(plan, scale, mask, grad_pre, point, spread, value, order):
    return pl.pallas_call(
        functools.partial(depth_grad_kernel, plan, scale),
        out_shape=[
            jax.ShapeDtypeStruct((SLOTS, 32, plan.width), bf16),
            jax.ShapeDtypeStruct((GROUP * plan.branches, plan.tile, 128), bf16),
        ],
        in_specs=[SMEM] + [VMEM] * 5,
        out_specs=[VMEM] * 2,
        scratch_shapes=[
            pltpu.VMEM((plan.lanes, plan.pixels, 128), f32),
            pltpu.VMEM((32, plan.width), f32),
            pltpu.VMEM((plan.pixels, plan.width), f32),
        ],
        compiler_params=pltpu.CompilerParams(vmem_limit_bytes=24 << 20),
        cost_estimate=pl.CostEstimate(flops=1 << 26, bytes_accessed=1 << 24, transcendentals=0),
        name="depth_grad",
    )(mask, grad_pre, point, spread, value, order)


def chip_sum_kernel(keep_ref, other_ref, *out_refs):
    _, _, chip, _ = whereabouts()
    for hop in range(CHIPS):
        out_refs[hop][...] = (keep_ref[chip ^ hop].astype(f32) + other_ref[chip ^ hop].astype(f32)).astype(bf16)


def chip_sum(keep, other):
    return pl.pallas_call(
        chip_sum_kernel,
        out_shape=[jax.ShapeDtypeStruct(keep.shape[1:], bf16)] * CHIPS,
        in_specs=[VMEM] * 2,
        out_specs=[VMEM] * CHIPS,
        compiler_params=pltpu.CompilerParams(vmem_limit_bytes=16 << 20),
        name="chip_sum",
    )(keep, other)


def plane_sum_kernel(plan, mask_ref, depth_ref, *refs):
    total, out_refs = refs[-1], refs[CHIPS:-1]
    plane, _, _, _ = whereabouts()
    slots, _ = slots_of(mask_ref, plan.branches)
    added = refs[0][...].astype(f32)
    for ref in refs[1:CHIPS]:
        added = added + ref[...].astype(f32)
    total[...] = added
    rows = plan.grad_rows
    for hop in range(plan.branches):
        slot = pick(slots, plane ^ hop)
        out_refs[hop][0:rows] = total[pl.ds(pl.multiple_of(slot * rows, 32), rows)].astype(bf16)
        out_refs[hop][rows:] = depth_ref[slot]


def plane_sum(plan, mask, depth, parts):
    return pl.pallas_call(
        functools.partial(plane_sum_kernel, plan),
        out_shape=[jax.ShapeDtypeStruct((plan.grad_rows + depth.shape[1], plan.width), bf16)] * plan.branches,
        in_specs=[SMEM] + [VMEM] * (1 + CHIPS),
        out_specs=[VMEM] * plan.branches,
        scratch_shapes=[pltpu.VMEM(parts[0].shape, f32)],
        compiler_params=pltpu.CompilerParams(vmem_limit_bytes=16 << 20),
        name="plane_sum",
    )(mask, depth, *parts)


def place_grads_kernel(plan, mask_ref, *refs):
    chunk_refs, (joining_ref, point_ref, depth_ref) = refs[:GROUP], refs[GROUP + 1:]
    plane, _, chip, core = whereabouts()
    active = pick([mask_ref[branch] for branch in range(plan.branches)], plane) > 0
    rows = plan.grad_rows
    taps = None
    for flip in range(2):
        for hop in range(CHIPS):
            chunk = jnp.where(active, chunk_refs[flip * CHIPS + hop][...].astype(f32), 0.0)
            at = (core ^ flip) * CHIPS + (chip ^ hop)
            joining_ref[pl.ds(pl.multiple_of(at * plan.join_rows, plan.join_rows), plan.join_rows)] = chunk[:plan.join_rows]
            place = pl.multiple_of(at * plan.point_rows, plan.point_rows)
            point_ref[0, pl.ds(place, plan.point_rows)] = chunk[plan.join_rows:rows]
            taps = chunk[rows:] if taps is None else taps + chunk[rows:]
    for tap in range(9):
        for group in range(plan.lanes):
            row, lane = 2 * tap + group // 2, (group % 2) * 128
            depth_ref[0, tap:tap + 1, group * 128:(group + 1) * 128] = taps[row:row + 1, lane:lane + 128]


def place_grads(plan, mask, chunks, token):
    return pl.pallas_call(
        functools.partial(place_grads_kernel, plan),
        out_shape=[
            jax.ShapeDtypeStruct((plan.width, plan.width), f32),
            jax.ShapeDtypeStruct((1, plan.chans, plan.width), f32),
            jax.ShapeDtypeStruct((1, 9, plan.chans), f32),
        ],
        in_specs=[SMEM] + [VMEM] * GROUP + [ANY],
        out_specs=[VMEM] * 3,
        compiler_params=pltpu.CompilerParams(vmem_limit_bytes=16 << 20),
        name="place_grads",
    )(mask, *chunks, token)


def per_device(features, cotangent, depth_weight, point_weight, joining_weight, branch_mask):
    row_count, col_count, chan_count = features.shape
    strips = lax.axis_size("strip")
    branches = lax.axis_size("branch")
    width = joining_weight.shape[1]
    plan = Plan(row_count, col_count, chan_count, width, branches)
    scale = 1.0 / math.sqrt(row_count * col_count * strips)
    groups = None if strips == GROUP else [list(range(g, g + GROUP)) for g in range(0, strips, GROUP)]

    def flip_strip(value, hop):
        return lax.ppermute(value, "strip", [(s, s ^ hop) for s in range(strips)])

    def flip_branch(value, hop):
        return lax.ppermute(value, "branch", [(b, b ^ hop) for b in range(branches)])

    def all_to_all(tiles):
        if groups is None:
            return lax.all_to_all(tiles, ("strip", "branch"), 0, 0, tiled=True)
        tiles = tiles.reshape(GROUP, branches, *tiles.shape[1:])
        tiles = lax.all_to_all(tiles, "branch", 1, 1, tiled=True)
        tiles = lax.all_to_all(tiles, "strip", 0, 0, tiled=True, axis_index_groups=groups)
        return tiles.reshape(GROUP * branches, *tiles.shape[2:])

    half = halve_weights(plan, point_weight, joining_weight)
    mine = [flip_branch(half, 1), flip_branch(half, 2)]
    mine.append(flip_branch(mine[1], 1))

    keep, send = spread_features(plan, features)
    joint = join_features(plan, keep, flip_strip(send, 1))
    pieces = [joint[0]] + [flip_strip(joint[hop], 2 * hop) for hop in range(1, CHIPS)]
    halos = []
    if groups is not None:
        strip = lax.axis_index("strip") % GROUP
        near = jnp.stack(pieces).reshape(CHIPS, 2, plan.piece, plan.chans)
        at = jnp.arange(GROUP)
        near = near[(at // 2) ^ (strip // 2), (at % 2) ^ (strip % 2)]
        down = [(s, s + GROUP) for s in range(strips - GROUP)]
        up = [(s + GROUP, s) for s in range(strips - GROUP)]
        halos = [lax.ppermute(near[GROUP - 4:], "strip", down), lax.ppermute(near[:4], "strip", up)]
    tiles = all_to_all(send_cotangent(plan, jnp.swapaxes(cotangent, 1, 2), depth_weight))
    dw_out, spread, pixel_cotangent, order, token = depthwise(plan, branch_mask, tiles, pieces, halos)

    mine, token = lax.optimization_barrier((mine, token))
    others = [flip_strip(value, 1) for value in mine]
    value, keep, send, grad_pre, points = main_step(
        plan, scale, branch_mask, dw_out, pixel_cotangent, point_weight, joining_weight, mine, others, token
    )
    parts = chip_sum(keep, flip_strip(send, 1))
    parts, value, grad_pre = lax.optimization_barrier((parts, value, grad_pre))
    parts = [parts[0]] + [flip_strip(parts[hop], 2 * hop) for hop in range(1, CHIPS)]
    taps, output_tiles = depth_grad(plan, scale, branch_mask, grad_pre, points, spread, value, order)
    output, token = place_output(plan, all_to_all(output_tiles))
    shares = plane_sum(plan, branch_mask, taps, parts)
    shares = [shares[0]] + [flip_branch(shares[hop], hop) for hop in range(1, branches)]
    share = sum(value.astype(f32) for value in shares)
    if groups is not None:
        peers = [list(range(s, strips, GROUP)) for s in range(GROUP)]
        share = lax.psum(share, "strip", axis_index_groups=peers)
    share = share.astype(bf16)
    chunks = [share] + [flip_strip(share, 2 * hop) for hop in range(1, CHIPS)]
    chunks = chunks + [flip_strip(chunk, 1) for chunk in chunks]
    joining_total, point_total, depth_total = place_grads(plan, branch_mask, chunks, token)
    return (jnp.swapaxes(output, 1, 2), joining_total, point_total, depth_total)


def solution(mesh):
    placed = (
        P("strip", None, None),
        P("strip", None, "branch"),
        P("branch", None, None),
        P("branch", None, None),
        P("branch", None),
        P(),
    )
    return jax.shard_map(
        per_device,
        mesh=mesh,
        in_specs=placed,
        out_specs=(
            P("strip", None, "branch"),
            P("branch", None),
            P("branch", None, None),
            P("branch", None, None),
        ),
        check_vma=False,
    )
```
